32 devices in a mesh: mem: 2 (over x), lat: 2 (over y), lon: 8 (over z, core).
Axes of the slice: x: 2, y: 2, z: 4, core: 2. Of those that a mesh axis runs over, the one named last changes fastest.
Arguments:
- members: float32 [2, 87, 16, 1024], P('mem', None, 'lat', 'lon'), may hold values from -6 to 6
- target: float32 [87, 16, 1024], P(None, 'lat', 'lon'), may hold values from -6 to 6
Outputs:
- gradient: float32 [2, 87, 16, 1024], P('mem', None, 'lat', 'lon')
- loss: float32 [], replicated
The draws below stay inside these ranges and needn't reach their ends.
All inputs are finite; a program needn't handle non-finite values.
Results may differ from the reference program's by a relative error of at most 0.0001.
Values sent between devices are 32-bit elements; how exact they have to be, the bound alone decides.
A program may use at most 64 MiB of HBM per device.

```python
import jax
import jax.numpy as jnp
from jax import lax

C = 87
LEVELS = 7
NLAT = 16
NLON = 1024


def draw_fields(key, leading):
    row_index = jnp.arange(NLAT, dtype=jnp.float32)
    col_index = jnp.arange(NLON, dtype=jnp.float32)
    smooth = jnp.zeros(leading + (NLAT, NLON), jnp.float32)
    for wave in range(4):
        wave_key = jax.random.fold_in(key, 11 + wave)
        keys = jax.random.split(wave_key, 5)
        amplitude = 0.4 * jax.random.normal(keys[0], leading, jnp.float32)
        zonal = jax.random.randint(keys[1], leading, 1, 7).astype(jnp.float32)
        meridional = jax.random.uniform(keys[2], leading, jnp.float32, 0.5, 3.0)
        phase_lon = jax.random.uniform(keys[3], leading, jnp.float32, -jnp.pi, jnp.pi)
        phase_lat = jax.random.uniform(keys[4], leading, jnp.float32, -jnp.pi, jnp.pi)
        lon_wave = jnp.cos(2.0 * jnp.pi * zonal[..., None] * col_index / NLON + phase_lon[..., None])
        lat_wave = jnp.cos(jnp.pi * meridional[..., None] * row_index / NLAT + phase_lat[..., None])
        smooth = smooth + amplitude[..., None, None] * lat_wave[..., :, None] * lon_wave[..., None, :]
    scale_key = jax.random.fold_in(key, 31)
    channel_scale = jnp.exp(jax.random.uniform(scale_key, leading, jnp.float32, jnp.log(0.3), jnp.log(3.0)))
    rough_key = jax.random.fold_in(key, 41)
    rough = jnp.clip(jax.random.normal(rough_key, leading + (NLAT, NLON), jnp.float32), -3.5, 3.5)
    values = channel_scale[..., None, None] * (smooth + rough)
    return jnp.clip(values, -6.0, 6.0)


def draw_members(key, part):
    return draw_fields(jax.random.fold_in(key, 101), (2, C))


def draw_target(key, part):
    return draw_fields(jax.random.fold_in(key, 202), (C,))


def setup_inputs(seed: int = 0) -> dict:
    splits = jax.random.split(jax.random.key(seed), 3)
    return {
        "members": draw_members(jax.random.fold_in(splits[2], 71), 0),
        "target": draw_target(jax.random.fold_in(splits[2], 71), 0),
    }


smooth_eps = 0.05

def soft_abs(values):
    return jnp.sqrt(values * values + smooth_eps * smooth_eps)

def lat_weights(row_count):
    row_index = jnp.arange(row_count, dtype=jnp.float32)
    return jnp.cos((89.875 - 0.25 * row_index) * (jnp.pi / 180.0))

def box_weights():
    current = lat_weights(NLAT)
    boxes = [current]
    for level in range(LEVELS):
        reach = 2 ** level
        current = current + jnp.pad(current, (0, reach))[reach:reach + NLAT]
        boxes.append(current)
    return boxes

def rows_ahead(values, reach):
    widths = [(0, 0)] * (values.ndim - 2) + [(0, reach), (0, 0)]
    return jnp.pad(values, widths)[..., reach:reach + NLAT, :]

def channel_loss(pair, truth):
    boxes = box_weights()
    box_sum = boxes[0][:, None] * (pair - truth[None])
    loss_total = jnp.zeros((), jnp.float32)
    for scale in range(LEVELS + 1):
        if scale > 0:
            reach = 2 ** (scale - 1)
            box_sum = box_sum + rows_ahead(box_sum, reach)
            box_sum = box_sum + jnp.roll(box_sum, -reach, axis=-1)
        lat_box = boxes[scale]
        pooled = box_sum / (2.0 ** scale * lat_box)[:, None]
        leader = pooled[0]
        partner = pooled[1]
        score = 0.5 * (soft_abs(leader) + soft_abs(partner)) - 0.5 * soft_abs(leader - partner)
        loss_total = loss_total + jnp.sum(lat_box[:, None] * score) / (NLON * jnp.sum(lat_box))
    return loss_total

def reference(members, target):

    def per_channel(inputs):
        return jax.value_and_grad(channel_loss)(inputs[0], inputs[1])
    channel_values, channel_grads = lax.map(per_channel, (jnp.moveaxis(members, 1, 0), target))
    loss = jnp.sum(channel_values) / C
    gradient = jnp.moveaxis(channel_grads, 0, 1) * (NLAT * NLON)
    return (gradient, loss)
```

```python
import functools

import jax
import jax.numpy as jnp
import numpy as np
from jax import lax
from jax.experimental import pallas as pl
from jax.experimental.pallas import tpu as pltpu
from jax.sharding import PartitionSpec as P

LEVELS = 7
SMOOTH_EPS = 0.05
CHUNKS = 2
MESH = pl.DeviceIdType.MESH


def lat_tables(row_count):
    row_index = np.arange(row_count, dtype=np.float32)
    angle = (np.float32(89.875) - np.float32(0.25) * row_index) * np.float32(np.pi / 180.0)
    current = np.cos(angle).astype(np.float32)
    boxes = [current]
    for level in range(LEVELS):
        reach = 2**level
        current = current + np.pad(current, (0, reach))[reach : reach + row_count]
        boxes.append(current)
    return boxes


def kernel(
    sizes, factors, members_ref, target_ref, tables_ref, grad_ref, loss_ref,
    mem_v, tgt_v, tab_v, sent, field, east, own_adj, east_adj, west_adj, final,
    total, group_loss, lon_loss,
    in_sem, x_send, x_recv, h_send, h_recv, b_send, b_recv, o_send, o_recv, o_own,
    lg_send, lg_recv, ll_send, ll_recv,
):
    channels, rows, cols, bands, sectors, span, chunks = sizes
    group = 2 * bands
    quota = span * chunks
    scales = LEVELS + 1
    mem, lat, lon = lax.axis_index("mem"), lax.axis_index("lat"), lax.axis_index("lon")
    me = mem * bands + lat

    def peer(offset):
        index = lax.rem(me + offset, group)
        return index, {"mem": index // bands, "lat": lax.rem(index, bands), "lon": lon}

    def sector(offset):
        return {"mem": mem, "lat": lat, "lon": lax.rem(lon + offset, sectors)}

    loads = [
        pltpu.make_async_copy(members_ref.at[0], mem_v, in_sem.at[0]),
        pltpu.make_async_copy(target_ref, tgt_v, in_sem.at[1]),
        pltpu.make_async_copy(tables_ref, tab_v, in_sem.at[2]),
    ]
    for load in loads:
        load.start()
    barrier = pltpu.get_barrier_semaphore()
    for offset in range(1, group):
        pl.semaphore_signal(barrier, inc=1, device_id=peer(offset)[1], device_id_type=MESH)
    for offset in range(1, sectors):
        pl.semaphore_signal(barrier, inc=1, device_id=sector(offset), device_id_type=MESH)
    for load in loads:
        load.wait()

    def inverse(scale, band):
        return tab_v[scale * bands + band]

    def loss_weight(scale, band):
        return tab_v[(scales + scale) * bands + band]

    def lat_weight(band):
        return tab_v[2 * scales * bands + band]

    own_weight = tab_v[2 * scales * bands + lat]

    def remote(source, target, send, recv, device):
        return pltpu.make_async_remote_copy(
            src_ref=source, dst_ref=target, send_sem=send, recv_sem=recv,
            device_id=device, device_id_type=MESH,
        )

    exchange = []
    for k in range(chunks):
        for g in range(group):
            base = g * quota + k * span
            valid = min(max(channels - base, 0), span)
            if valid > 0:
                part = mem_v[base : base + valid] - tgt_v[base : base + valid]
                sent[k, g, 0:valid] = part * own_weight
            if valid < span:
                sent[k, g, valid:span] = jnp.zeros((span - valid, rows, cols), jnp.float32)
        if k == 0:
            pl.semaphore_wait(barrier, group + sectors - 2)
        copies = []
        for offset in range(1, group):
            index, device = peer(offset)
            copy = remote(sent.at[k, index], field.at[k, me], x_send.at[k, offset], x_recv.at[k, offset], device)
            copy.start()
            copies.append(copy)
        field[k, me] = sent[k, me]
        exchange.append(copies)

    halos = []
    for k in range(chunks):
        for copy in exchange[k]:
            copy.wait_recv()
        copy = remote(field.at[k], east.at[k], h_send.at[k], h_recv.at[k], sector(sectors - 1))
        copy.start()
        halos.append(copy)

    lane = lax.broadcasted_iota(jnp.int32, (rows, cols), 1)
    sub = lax.broadcasted_iota(jnp.int32, (rows, cols), 0)
    zero = jnp.zeros((rows, cols), jnp.float32)

    def rows_ahead(tiles, reach):
        hops, remain = divmod(reach, rows)
        if hops >= bands:
            return tiles
        at = lambda b: tiles[b] if b < bands else None
        if remain == 0:
            return [t if at(b + hops) is None else t + at(b + hops) for b, t in enumerate(tiles)]
        turned = [pltpu.roll(t, rows - remain, 0) for t in tiles]
        near = sub < rows - remain
        out = []
        for b, t in enumerate(tiles):
            if b + hops >= bands:
                out.append(t)
                continue
            beyond = turned[b + hops + 1] if b + hops + 1 < bands else zero
            out.append(t + jnp.where(near, turned[b + hops], beyond))
        return out

    def rows_behind(tiles, reach):
        hops, remain = divmod(reach, rows)
        if hops >= bands:
            return tiles
        if remain == 0:
            return [t + tiles[b - hops] if b >= hops else t for b, t in enumerate(tiles)]
        turned = [pltpu.roll(t, remain, 0) for t in tiles]
        near = sub >= remain
        out = []
        for b, t in enumerate(tiles):
            if b < hops:
                out.append(t)
                continue
            beyond = turned[b - hops - 1] if b - hops - 1 >= 0 else zero
            out.append(t + jnp.where(near, turned[b - hops], beyond))
        return out

    def absolute(value):
        square = value * value + SMOOTH_EPS * SMOOTH_EPS
        root = lax.rsqrt(square)
        return square * root, value * root

    total[...] = zero

    def work(k, i):
        own = [[field[k, m * bands + b, i] for b in range(bands)] for m in range(2)]
        next_ = [[east[k, m * bands + b, i] for b in range(bands)] for m in range(2)]
        slopes = []
        score = zero
        for scale in range(scales):
            if scale > 0:
                reach = 2 ** (scale - 1)
                own = [rows_ahead(t, reach) for t in own]
                next_ = [rows_ahead(t, reach) for t in next_]
                keep = lane < cols - reach
                for m in range(2):
                    for b in range(bands):
                        turned_own = pltpu.roll(own[m][b], cols - reach, 1)
                        turned_next = pltpu.roll(next_[m][b], cols - reach, 1)
                        own[m][b] = own[m][b] + jnp.where(keep, turned_own, turned_next)
                        if scale < LEVELS:
                            next_[m][b] = next_[m][b] + turned_next
            slope = [[], []]
            for b in range(bands):
                leader = own[0][b] * inverse(scale, b)
                partner = own[1][b] * inverse(scale, b)
                first_abs, first_slope = absolute(leader)
                second_abs, second_slope = absolute(partner)
                spread_abs, spread_slope = absolute(leader - partner)
                score = score + loss_weight(scale, b) * (first_abs + second_abs - spread_abs)
                slope[0].append((first_slope - spread_slope) * factors[scale])
                slope[1].append((second_slope + spread_slope) * factors[scale])
            slopes.append(slope)
        mine = slopes[LEVELS]
        theirs = [[zero] * bands for m in range(2)]
        for level in reversed(range(LEVELS)):
            reach = 2**level
            keep = lane >= reach
            for m in range(2):
                for b in range(bands):
                    turned_mine = pltpu.roll(mine[m][b], reach, 1)
                    if level == LEVELS - 1:
                        theirs[m][b] = jnp.where(keep, zero, turned_mine)
                    else:
                        turned_theirs = pltpu.roll(theirs[m][b], reach, 1)
                        theirs[m][b] = theirs[m][b] + jnp.where(keep, turned_theirs, turned_mine)
                    mine[m][b] = mine[m][b] + jnp.where(keep, turned_mine, zero)
            mine = [rows_behind(t, reach) for t in mine]
            theirs = [rows_behind(t, reach) for t in theirs]
            mine = [[t + s for t, s in zip(mine[m], slopes[level][m])] for m in range(2)]
        for m in range(2):
            for b in range(bands):
                own_adj[k, m * bands + b, i] = mine[m][b]
                east_adj[k, m * bands + b, i] = theirs[m][b]
        valid = (me * quota + k * span + i < channels).astype(jnp.float32)
        total[...] += score * valid

    def finish(k, back):
        back.wait_recv()
        for g in range(group):
            final[k, g] = (own_adj[k, g] + west_adj[k, g]) * lat_weight(g % bands)
        place = pl.ds(me * quota + k * span, span)
        copies = []
        for offset in range(1, group):
            index, device = peer(offset)
            copy = remote(final.at[k, index], grad_ref.at[place], o_send.at[k, offset], o_recv.at[k, offset], device)
            copy.start()
            copies.append(copy)
        stay = pltpu.make_async_copy(final.at[k, me], grad_ref.at[place], o_own.at[k])
        stay.start()
        return copies, stay

    backs, outs = [], []
    for k in range(chunks):
        halos[k].wait_recv()

        def step(i, carry, k=k):
            work(k, i)
            return carry

        lax.fori_loop(0, span, step, 0)
        back = remote(east_adj.at[k], west_adj.at[k], b_send.at[k], b_recv.at[k], sector(1))
        back.start()
        backs.append(back)
        if k > 0:
            outs.append(finish(k - 1, backs[k - 1]))

    group_loss[me] = total[...]
    group_copies = []
    for offset in range(1, group):
        copy = remote(total, group_loss.at[me], lg_send.at[offset], lg_recv.at[offset], peer(offset)[1])
        copy.start()
        group_copies.append(copy)
    outs.append(finish(chunks - 1, backs[chunks - 1]))
    for copy in group_copies:
        copy.wait()
    subtotal = group_loss[0]
    for g in range(1, group):
        subtotal = subtotal + group_loss[g]
    lon_loss[lon] = subtotal
    total[...] = subtotal
    lon_copies = []
    for offset in range(1, sectors):
        copy = remote(total, lon_loss.at[lon], ll_send.at[offset], ll_recv.at[offset], sector(offset))
        copy.start()
        lon_copies.append(copy)
    for copy in lon_copies:
        copy.wait()
    subtotal = lon_loss[0]
    for j in range(1, sectors):
        subtotal = subtotal + lon_loss[j]
    loss_ref[0, 0] = jnp.sum(subtotal)

    for copies in exchange:
        for copy in copies:
            copy.wait_send()
    for copy in halos + backs:
        copy.wait_send()
    for copies, stay in outs:
        stay.wait()
        for copy in copies:
            copy.wait()


def shards(members, target):
    channels, rows, cols = target.shape
    bands, sectors = lax.axis_size("lat"), lax.axis_size("lon")
    assert lax.axis_size("mem") == 2 and cols >= 2**LEVELS
    group = 2 * bands
    chunks = CHUNKS
    span = -(-channels // (group * chunks))
    quota = span * chunks
    scales = LEVELS + 1
    nlat, nlon = rows * bands, cols * sectors

    boxes = lat_tables(nlat)
    sums = [float(np.sum(box.astype(np.float64))) for box in boxes]
    inverses = [1.0 / (2.0**s * boxes[s].astype(np.float64)) for s in range(scales)]
    weights = [0.5 * boxes[s].astype(np.float64) / (channels * nlon * sums[s]) for s in range(scales)]
    vectors = np.stack(inverses + weights + [boxes[0].astype(np.float64)]).astype(np.float32)
    tables = np.broadcast_to(vectors.reshape(-1, rows, 1), ((2 * scales + 1) * bands, rows, cols))
    factors = [0.5 * nlat / (sums[s] * 2.0**s) for s in range(scales)]

    sizes = (channels, rows, cols, bands, sectors, span, chunks)
    blocks = pltpu.VMEM((chunks, group, span, rows, cols), jnp.float32)
    dma = pltpu.SemaphoreType.DMA
    gradient, loss = pl.pallas_call(
        functools.partial(kernel, sizes, factors),
        out_shape=(
            jax.ShapeDtypeStruct((group * quota, rows, cols), jnp.float32),
            jax.ShapeDtypeStruct((1, 1), jnp.float32),
        ),
        in_specs=[pl.BlockSpec(memory_space=pl.ANY)] * 3,
        out_specs=(pl.BlockSpec(memory_space=pl.ANY), pl.BlockSpec(memory_space=pltpu.SMEM)),
        scratch_shapes=[
            pltpu.VMEM((channels, rows, cols), jnp.float32),
            pltpu.VMEM((channels, rows, cols), jnp.float32),
            pltpu.VMEM(tables.shape, jnp.float32),
            blocks, blocks, blocks, blocks, blocks, blocks, blocks,
            pltpu.VMEM((rows, cols), jnp.float32),
            pltpu.VMEM((group, rows, cols), jnp.float32),
            pltpu.VMEM((sectors, rows, cols), jnp.float32),
            dma((3,)),
            dma((chunks, group)), dma((chunks, group)),
            dma((chunks,)), dma((chunks,)),
            dma((chunks,)), dma((chunks,)),
            dma((chunks, group)), dma((chunks, group)), dma((chunks,)),
            dma((group,)), dma((group,)),
            dma((sectors,)), dma((sectors,)),
        ],
        compiler_params=pltpu.CompilerParams(
            collective_id=0, has_side_effects=True, vmem_limit_bytes=32 * 1024 * 1024
        ),
    )(members, target, jnp.asarray(tables))
    return gradient[None, :channels], loss[0, 0]


def solution(mesh):
    return jax.shard_map(
        shards,
        mesh=mesh,
        in_specs=(P("mem", None, "lat", "lon"), P(None, "lat", "lon")),
        out_specs=(P("mem", None, "lat", "lon"), P()),
        check_vma=False,
    )
```

```python
import functools

import jax
import jax.numpy as jnp
import numpy as np
from jax import lax
from jax.experimental import pallas as pl
from jax.experimental.pallas import tpu as pltpu
from jax.sharding import PartitionSpec as P

LEVELS = 7
SMOOTH_EPS = 0.05
CHUNKS = 2
MESH = pl.DeviceIdType.MESH


def lat_tables(row_count):
    row_index = np.arange(row_count, dtype=np.float32)
    angle = (np.float32(89.875) - np.float32(0.25) * row_index) * np.float32(np.pi / 180.0)
    current = np.cos(angle).astype(np.float32)
    boxes = [current]
    for level in range(LEVELS):
        reach = 2**level
        current = current + np.pad(current, (0, reach))[reach : reach + row_count]
        boxes.append(current)
    return boxes


def kernel(
    sizes, factors, vectors, members_ref, target_ref, grad_ref, loss_ref,
    mem_v, tgt_v, tab_v, slopes, sent, field, east, own_adj, east_adj, west_adj, final,
    total, group_loss, lon_loss,
    in_sem, x_send, x_recv, h_send, h_recv, b_send, b_recv, o_send, o_recv, o_own,
    lg_send, lg_recv, ll_send, ll_recv,
):
    channels, rows, cols, bands, sectors, span, chunks = sizes
    group = 2 * bands
    quota = span * chunks
    scales = LEVELS + 1
    mem, lat, lon = lax.axis_index("mem"), lax.axis_index("lat"), lax.axis_index("lon")
    me = mem * bands + lat

    def peer(offset):
        index = lax.rem(me + offset, group)
        return index, {"mem": index // bands, "lat": lax.rem(index, bands), "lon": lon}

    def sector(offset):
        return {"mem": mem, "lat": lat, "lon": lax.rem(lon + offset, sectors)}

    loads = [
        pltpu.make_async_copy(members_ref.at[0], mem_v, in_sem.at[0]),
        pltpu.make_async_copy(target_ref, tgt_v, in_sem.at[1]),
    ]
    for load in loads:
        load.start()
    barrier = pltpu.get_barrier_semaphore()
    for offset in range(1, group):
        pl.semaphore_signal(barrier, inc=1, device_id=peer(offset)[1], device_id_type=MESH)
    for offset in range(1, sectors):
        pl.semaphore_signal(barrier, inc=1, device_id=sector(offset), device_id_type=MESH)

    lane = lax.broadcasted_iota(jnp.int32, (rows, cols), 1)
    sub = lax.broadcasted_iota(jnp.int32, (rows, cols), 0)
    zero = jnp.zeros((rows, cols), jnp.float32)
    for i, vector in enumerate(vectors):
        tile = jnp.full((rows, cols), vector[0], jnp.float32)
        for r in range(1, rows):
            tile = jnp.where(sub == r, vector[r], tile)
        tab_v[i] = tile
    for load in loads:
        load.wait()

    def inverse(scale, band):
        return tab_v[scale * bands + band]

    def loss_weight(scale, band):
        return tab_v[(scales + scale) * bands + band]

    def lat_weight(band):
        return tab_v[2 * scales * bands + band]

    own_weight = tab_v[2 * scales * bands + lat]

    def remote(source, target, send, recv, device):
        return pltpu.make_async_remote_copy(
            src_ref=source, dst_ref=target, send_sem=send, recv_sem=recv,
            device_id=device, device_id_type=MESH,
        )

    exchange = []
    for k in range(chunks):
        for g in range(group):
            base = g * quota + k * span
            valid = min(max(channels - base, 0), span)
            if valid > 0:
                part = mem_v[base : base + valid] - tgt_v[base : base + valid]
                sent[k, g, 0:valid] = part * own_weight
            if valid < span:
                sent[k, g, valid:span] = jnp.zeros((span - valid, rows, cols), jnp.float32)
        if k == 0:
            pl.semaphore_wait(barrier, group + sectors - 2)
        copies = []
        for offset in range(1, group):
            index, device = peer(offset)
            copy = remote(sent.at[k, index], field.at[k, me], x_send.at[k, offset], x_recv.at[k, offset], device)
            copy.start()
            copies.append(copy)
        field[k, me] = sent[k, me]
        exchange.append(copies)

    halos = []
    for k in range(chunks):
        for copy in exchange[k]:
            copy.wait_recv()
        copy = remote(field.at[k], east.at[k], h_send.at[k], h_recv.at[k], sector(sectors - 1))
        copy.start()
        halos.append(copy)

    def rows_ahead(tiles, reach):
        hops, remain = divmod(reach, rows)
        if hops >= bands:
            return tiles
        at = lambda b: tiles[b] if b < bands else None
        if remain == 0:
            return [t if at(b + hops) is None else t + at(b + hops) for b, t in enumerate(tiles)]
        turned = [pltpu.roll(t, rows - remain, 1) for t in tiles]
        near = sub < rows - remain
        out = []
        for b, t in enumerate(tiles):
            if b + hops >= bands:
                out.append(t)
                continue
            beyond = turned[b + hops + 1] if b + hops + 1 < bands else zero
            out.append(t + jnp.where(near, turned[b + hops], beyond))
        return out

    def rows_behind(tiles, reach):
        hops, remain = divmod(reach, rows)
        if hops >= bands:
            return tiles
        if remain == 0:
            return [t + tiles[b - hops] if b >= hops else t for b, t in enumerate(tiles)]
        turned = [pltpu.roll(t, remain, 1) for t in tiles]
        near = sub >= remain
        out = []
        for b, t in enumerate(tiles):
            if b < hops:
                out.append(t)
                continue
            beyond = turned[b - hops - 1] if b - hops - 1 >= 0 else zero
            out.append(t + jnp.where(near, turned[b - hops], beyond))
        return out

    def absolute(value):
        square = value * value + SMOOTH_EPS * SMOOTH_EPS
        root = lax.rsqrt(square)
        return square * root, value * root

    total[...] = zero

    def work(k):
        own = [[field[k, m * bands + b] for b in range(bands)] for m in range(2)]
        next_ = [[east[k, m * bands + b] for b in range(bands)] for m in range(2)]
        score = jnp.zeros((span, rows, cols), jnp.float32)
        for scale in range(scales):
            if scale > 0:
                reach = 2 ** (scale - 1)
                own = [rows_ahead(t, reach) for t in own]
                next_ = [rows_ahead(t, reach) for t in next_]
                keep = lane < cols - reach
                for m in range(2):
                    for b in range(bands):
                        turned_own = pltpu.roll(own[m][b], cols - reach, 2)
                        turned_next = pltpu.roll(next_[m][b], cols - reach, 2)
                        own[m][b] = own[m][b] + jnp.where(keep, turned_own, turned_next)
                        if scale < LEVELS:
                            next_[m][b] = next_[m][b] + turned_next
            for b in range(bands):
                leader = own[0][b] * inverse(scale, b)
                partner = own[1][b] * inverse(scale, b)
                first_abs, first_slope = absolute(leader)
                second_abs, second_slope = absolute(partner)
                spread_abs, spread_slope = absolute(leader - partner)
                score = score + loss_weight(scale, b) * (first_abs + second_abs - spread_abs)
                slopes[scale, b] = (first_slope - spread_slope) * factors[scale]
                slopes[scale, bands + b] = (second_slope + spread_slope) * factors[scale]
        mine = [[slopes[LEVELS, m * bands + b] for b in range(bands)] for m in range(2)]
        theirs = [[None] * bands for m in range(2)]
        for level in reversed(range(LEVELS)):
            reach = 2**level
            keep = lane >= reach
            for m in range(2):
                for b in range(bands):
                    turned_mine = pltpu.roll(mine[m][b], reach, 2)
                    if level == LEVELS - 1:
                        theirs[m][b] = jnp.where(keep, zero, turned_mine)
                    else:
                        turned_theirs = pltpu.roll(theirs[m][b], reach, 2)
                        theirs[m][b] = theirs[m][b] + jnp.where(keep, turned_theirs, turned_mine)
                    mine[m][b] = mine[m][b] + jnp.where(keep, turned_mine, zero)
            mine = [rows_behind(t, reach) for t in mine]
            theirs = [rows_behind(t, reach) for t in theirs]
            mine = [[mine[m][b] + slopes[level, m * bands + b] for b in range(bands)] for m in range(2)]
        for m in range(2):
            for b in range(bands):
                own_adj[k, m * bands + b] = mine[m][b]
                east_adj[k, m * bands + b] = theirs[m][b]
        part = zero
        for i in range(span):
            place = k * span + i
            if (group - 1) * quota + place < channels:
                part = part + score[i]
            else:
                part = part + score[i] * (me * quota + place < channels).astype(jnp.float32)
        total[...] += part

    def finish(k, back):
        back.wait_recv()
        for g in range(group):
            final[k, g] = (own_adj[k, g] + west_adj[k, g]) * lat_weight(g % bands)
        place = pl.ds(me * quota + k * span, span)
        copies = []
        for offset in range(1, group):
            index, device = peer(offset)
            copy = remote(final.at[k, index], grad_ref.at[place], o_send.at[k, offset], o_recv.at[k, offset], device)
            copy.start()
            copies.append(copy)
        stay = pltpu.make_async_copy(final.at[k, me], grad_ref.at[place], o_own.at[k])
        stay.start()
        return copies, stay

    backs, outs = [], []
    for k in range(chunks):
        halos[k].wait_recv()

        work(k)
        back = remote(east_adj.at[k], west_adj.at[k], b_send.at[k], b_recv.at[k], sector(1))
        back.start()
        backs.append(back)
        if k > 0:
            outs.append(finish(k - 1, backs[k - 1]))

    group_loss[me] = total[...]
    group_copies = []
    for offset in range(1, group):
        copy = remote(total, group_loss.at[me], lg_send.at[offset], lg_recv.at[offset], peer(offset)[1])
        copy.start()
        group_copies.append(copy)
    outs.append(finish(chunks - 1, backs[chunks - 1]))
    for copy in group_copies:
        copy.wait()
    subtotal = group_loss[0]
    for g in range(1, group):
        subtotal = subtotal + group_loss[g]
    lon_loss[lon] = subtotal
    total[...] = subtotal
    lon_copies = []
    for offset in range(1, sectors):
        copy = remote(total, lon_loss.at[lon], ll_send.at[offset], ll_recv.at[offset], sector(offset))
        copy.start()
        lon_copies.append(copy)
    for copy in lon_copies:
        copy.wait()
    subtotal = lon_loss[0]
    for j in range(1, sectors):
        subtotal = subtotal + lon_loss[j]
    loss_ref[0, 0] = jnp.sum(subtotal)

    for copies in exchange:
        for copy in copies:
            copy.wait_send()
    for copy in halos + backs:
        copy.wait_send()
    for copies, stay in outs:
        stay.wait()
        for copy in copies:
            copy.wait()


def shards(members, target):
    channels, rows, cols = target.shape
    bands, sectors = lax.axis_size("lat"), lax.axis_size("lon")
    assert lax.axis_size("mem") == 2 and cols >= 2**LEVELS
    group = 2 * bands
    chunks = CHUNKS
    span = -(-channels // (group * chunks))
    quota = span * chunks
    scales = LEVELS + 1
    nlat, nlon = rows * bands, cols * sectors

    boxes = lat_tables(nlat)
    sums = [float(np.sum(box.astype(np.float64))) for box in boxes]
    inverses = [1.0 / (2.0**s * boxes[s].astype(np.float64)) for s in range(scales)]
    weights = [0.5 * boxes[s].astype(np.float64) / (channels * nlon * sums[s]) for s in range(scales)]
    vectors = np.stack(inverses + weights + [boxes[0].astype(np.float64)]).reshape(-1, rows).tolist()
    factors = [0.5 * nlat / (sums[s] * 2.0**s) for s in range(scales)]

    sizes = (channels, rows, cols, bands, sectors, span, chunks)
    blocks = pltpu.VMEM((chunks, group, span, rows, cols), jnp.float32)
    dma = pltpu.SemaphoreType.DMA
    gradient, loss = pl.pallas_call(
        functools.partial(kernel, sizes, factors, vectors),
        out_shape=(
            jax.ShapeDtypeStruct((group * quota, rows, cols), jnp.float32),
            jax.ShapeDtypeStruct((1, 1), jnp.float32),
        ),
        in_specs=[pl.BlockSpec(memory_space=pl.ANY)] * 2,
        out_specs=(pl.BlockSpec(memory_space=pl.ANY), pl.BlockSpec(memory_space=pltpu.SMEM)),
        scratch_shapes=[
            pltpu.VMEM((channels, rows, cols), jnp.float32),
            pltpu.VMEM((channels, rows, cols), jnp.float32),
            pltpu.VMEM((len(vectors), rows, cols), jnp.float32),
            pltpu.VMEM((scales, group, span, rows, cols), jnp.float32),
            blocks, blocks, blocks, blocks, blocks, blocks, blocks,
            pltpu.VMEM((rows, cols), jnp.float32),
            pltpu.VMEM((group, rows, cols), jnp.float32),
            pltpu.VMEM((sectors, rows, cols), jnp.float32),
            dma((2,)),
            dma((chunks, group)), dma((chunks, group)),
            dma((chunks,)), dma((chunks,)),
            dma((chunks,)), dma((chunks,)),
            dma((chunks, group)), dma((chunks, group)), dma((chunks,)),
            dma((group,)), dma((group,)),
            dma((sectors,)), dma((sectors,)),
        ],
        compiler_params=pltpu.CompilerParams(
            collective_id=0, has_side_effects=True, vmem_limit_bytes=60 * 1024 * 1024
        ),
    )(members, target)
    return gradient[None, :channels], loss[0, 0]


def solution(mesh):
    return jax.shard_map(
        shards,
        mesh=mesh,
        in_specs=(P("mem", None, "lat", "lon"), P(None, "lat", "lon")),
        out_specs=(P("mem", None, "lat", "lon"), P()),
        check_vma=False,
    )
```

```python
import functools

import jax
import jax.numpy as jnp
import numpy as np
from jax import lax
from jax.experimental import pallas as pl
from jax.experimental.pallas import tpu as pltpu
from jax.sharding import PartitionSpec as P

LEVELS = 7
SMOOTH_EPS = 0.05
CHUNKS = 4
MESH = pl.DeviceIdType.MESH


def lat_tables(row_count):
    row_index = np.arange(row_count, dtype=np.float32)
    angle = (np.float32(89.875) - np.float32(0.25) * row_index) * np.float32(np.pi / 180.0)
    current = np.cos(angle).astype(np.float32)
    boxes = [current]
    for level in range(LEVELS):
        reach = 2**level
        current = current + np.pad(current, (0, reach))[reach : reach + row_count]
        boxes.append(current)
    return boxes


def kernel(
    sizes, factors, vectors, members_ref, target_ref, grad_ref, loss_ref,
    mem_v, tgt_v, tab_v, slopes, sent, field, east, own_adj, east_adj, west_adj, final,
    total, group_loss, lon_loss,
    in_sem, x_send, x_recv, h_send, h_recv, b_send, b_recv, o_send, o_recv, o_own,
    lg_send, lg_recv, ll_send, ll_recv,
):
    channels, rows, cols, bands, sectors, spans = sizes
    group = 2 * bands
    quota = sum(spans)
    chunks = len(spans)
    starts = [sum(spans[:k]) for k in range(chunks)]
    part = [pl.ds(start, span) for start, span in zip(starts, spans)]
    scales = LEVELS + 1
    mem, lat, lon = lax.axis_index("mem"), lax.axis_index("lat"), lax.axis_index("lon")
    me = mem * bands + lat

    def peer(offset):
        index = lax.rem(me + offset, group)
        return index, {"mem": index // bands, "lat": lax.rem(index, bands), "lon": lon}

    def sector(offset):
        return {"mem": mem, "lat": lat, "lon": lax.rem(lon + offset, sectors)}

    loads = [
        pltpu.make_async_copy(members_ref.at[0], mem_v, in_sem.at[0]),
        pltpu.make_async_copy(target_ref, tgt_v, in_sem.at[1]),
    ]
    for load in loads:
        load.start()
    barrier = pltpu.get_barrier_semaphore()
    for offset in range(1, group):
        pl.semaphore_signal(barrier, inc=1, device_id=peer(offset)[1], device_id_type=MESH)
    for offset in range(1, sectors):
        pl.semaphore_signal(barrier, inc=1, device_id=sector(offset), device_id_type=MESH)

    lane = lax.broadcasted_iota(jnp.int32, (rows, cols), 1)
    sub = lax.broadcasted_iota(jnp.int32, (rows, cols), 0)
    zero = jnp.zeros((rows, cols), jnp.float32)
    for i, vector in enumerate(vectors):
        tile = jnp.full((rows, cols), vector[0], jnp.float32)
        for r in range(1, rows):
            tile = jnp.where(sub == r, vector[r], tile)
        tab_v[i] = tile
    for load in loads:
        load.wait()

    def inverse(scale, band):
        return tab_v[scale * bands + band]

    def loss_weight(scale, band):
        return tab_v[(scales + scale) * bands + band]

    def lat_weight(band):
        return tab_v[2 * scales * bands + band]

    own_weight = tab_v[2 * scales * bands + lat]

    def remote(source, target, send, recv, device):
        return pltpu.make_async_remote_copy(
            src_ref=source, dst_ref=target, send_sem=send, recv_sem=recv,
            device_id=device, device_id_type=MESH,
        )

    exchange = []
    for k in range(chunks):
        for g in range(group):
            base = g * quota + starts[k]
            valid = min(max(channels - base, 0), spans[k])
            edge, stop = starts[k] + valid, starts[k] + spans[k]
            if valid > 0:
                difference = mem_v[base : base + valid] - tgt_v[base : base + valid]
                sent[g, starts[k] : edge] = difference * own_weight
            if edge < stop:
                sent[g, edge:stop] = jnp.zeros((stop - edge, rows, cols), jnp.float32)
        if k == 0:
            pl.semaphore_wait(barrier, group + sectors - 2)
        copies = []
        for offset in range(1, group):
            index, device = peer(offset)
            copy = remote(sent.at[index, part[k]], field.at[me, part[k]], x_send.at[k, offset], x_recv.at[k, offset], device)
            copy.start()
            copies.append(copy)
        field[me, part[k]] = sent[me, part[k]]
        exchange.append(copies)

    halos = []
    for k in range(chunks):
        for copy in exchange[k]:
            copy.wait_recv()
        copy = remote(field.at[:, part[k]], east.at[:, part[k]], h_send.at[k], h_recv.at[k], sector(sectors - 1))
        copy.start()
        halos.append(copy)

    def rows_ahead(tiles, reach):
        hops, remain = divmod(reach, rows)
        if hops >= bands:
            return tiles
        at = lambda b: tiles[b] if b < bands else None
        if remain == 0:
            return [t if at(b + hops) is None else t + at(b + hops) for b, t in enumerate(tiles)]
        turned = [pltpu.roll(t, rows - remain, 1) for t in tiles]
        near = sub < rows - remain
        out = []
        for b, t in enumerate(tiles):
            if b + hops >= bands:
                out.append(t)
                continue
            beyond = turned[b + hops + 1] if b + hops + 1 < bands else zero
            out.append(t + jnp.where(near, turned[b + hops], beyond))
        return out

    def rows_behind(tiles, reach):
        hops, remain = divmod(reach, rows)
        if hops >= bands:
            return tiles
        if remain == 0:
            return [t + tiles[b - hops] if b >= hops else t for b, t in enumerate(tiles)]
        turned = [pltpu.roll(t, remain, 1) for t in tiles]
        near = sub >= remain
        out = []
        for b, t in enumerate(tiles):
            if b < hops:
                out.append(t)
                continue
            beyond = turned[b - hops - 1] if b - hops - 1 >= 0 else zero
            out.append(t + jnp.where(near, turned[b - hops], beyond))
        return out

    def absolute(value):
        square = value * value + SMOOTH_EPS * SMOOTH_EPS
        root = lax.rsqrt(square)
        return square * root, value * root

    total[...] = zero

    def work(k):
        span = spans[k]
        own = [[field[m * bands + b, part[k]] for b in range(bands)] for m in range(2)]
        next_ = [[east[m * bands + b, part[k]] for b in range(bands)] for m in range(2)]
        score = jnp.zeros((span, rows, cols), jnp.float32)
        for scale in range(scales):
            if scale > 0:
                reach = 2 ** (scale - 1)
                own = [rows_ahead(t, reach) for t in own]
                next_ = [rows_ahead(t, reach) for t in next_]
                keep = lane < cols - reach
                for m in range(2):
                    for b in range(bands):
                        turned_own = pltpu.roll(own[m][b], cols - reach, 2)
                        turned_next = pltpu.roll(next_[m][b], cols - reach, 2)
                        own[m][b] = own[m][b] + jnp.where(keep, turned_own, turned_next)
                        if scale < LEVELS:
                            next_[m][b] = next_[m][b] + turned_next
            for b in range(bands):
                leader = own[0][b] * inverse(scale, b)
                partner = own[1][b] * inverse(scale, b)
                first_abs, first_slope = absolute(leader)
                second_abs, second_slope = absolute(partner)
                spread_abs, spread_slope = absolute(leader - partner)
                score = score + loss_weight(scale, b) * (first_abs + second_abs - spread_abs)
                slopes[scale, b, 0:span] = (first_slope - spread_slope) * factors[scale]
                slopes[scale, bands + b, 0:span] = (second_slope + spread_slope) * factors[scale]
        mine = [[slopes[LEVELS, m * bands + b, 0:span] for b in range(bands)] for m in range(2)]
        theirs = [[None] * bands for m in range(2)]
        for level in reversed(range(LEVELS)):
            reach = 2**level
            keep = lane >= reach
            for m in range(2):
                for b in range(bands):
                    turned_mine = pltpu.roll(mine[m][b], reach, 2)
                    if level == LEVELS - 1:
                        theirs[m][b] = jnp.where(keep, zero, turned_mine)
                    else:
                        turned_theirs = pltpu.roll(theirs[m][b], reach, 2)
                        theirs[m][b] = theirs[m][b] + jnp.where(keep, turned_theirs, turned_mine)
                    mine[m][b] = mine[m][b] + jnp.where(keep, turned_mine, zero)
            mine = [rows_behind(t, reach) for t in mine]
            theirs = [rows_behind(t, reach) for t in theirs]
            mine = [[mine[m][b] + slopes[level, m * bands + b, 0:span] for b in range(bands)] for m in range(2)]
        for m in range(2):
            for b in range(bands):
                own_adj[m * bands + b, part[k]] = mine[m][b]
                east_adj[m * bands + b, part[k]] = theirs[m][b]
        kept = zero
        for i in range(span):
            place = starts[k] + i
            if (group - 1) * quota + place < channels:
                kept = kept + score[i]
            else:
                kept = kept + score[i] * (me * quota + place < channels).astype(jnp.float32)
        total[...] += kept

    def finish(k, back):
        back.wait_recv()
        for g in range(group):
            final[g, part[k]] = (own_adj[g, part[k]] + west_adj[g, part[k]]) * lat_weight(g % bands)
        place = pl.ds(me * quota + starts[k], spans[k])
        copies = []
        for offset in range(1, group):
            index, device = peer(offset)
            copy = remote(final.at[index, part[k]], grad_ref.at[place], o_send.at[k, offset], o_recv.at[k, offset], device)
            copy.start()
            copies.append(copy)
        stay = pltpu.make_async_copy(final.at[me, part[k]], grad_ref.at[place], o_own.at[k])
        stay.start()
        return copies, stay

    backs, outs = [], []
    for k in range(chunks):
        halos[k].wait_recv()

        work(k)
        back = remote(east_adj.at[:, part[k]], west_adj.at[:, part[k]], b_send.at[k], b_recv.at[k], sector(1))
        back.start()
        backs.append(back)
        if k > 0:
            outs.append(finish(k - 1, backs[k - 1]))

    group_loss[me] = total[...]
    group_copies = []
    for offset in range(1, group):
        copy = remote(total, group_loss.at[me], lg_send.at[offset], lg_recv.at[offset], peer(offset)[1])
        copy.start()
        group_copies.append(copy)
    outs.append(finish(chunks - 1, backs[chunks - 1]))
    for copy in group_copies:
        copy.wait()
    subtotal = group_loss[0]
    for g in range(1, group):
        subtotal = subtotal + group_loss[g]
    lon_loss[lon] = subtotal
    total[...] = subtotal
    lon_copies = []
    for offset in range(1, sectors):
        copy = remote(total, lon_loss.at[lon], ll_send.at[offset], ll_recv.at[offset], sector(offset))
        copy.start()
        lon_copies.append(copy)
    for copy in lon_copies:
        copy.wait()
    subtotal = lon_loss[0]
    for j in range(1, sectors):
        subtotal = subtotal + lon_loss[j]
    loss_ref[0, 0] = jnp.sum(subtotal)

    for copies in exchange:
        for copy in copies:
            copy.wait_send()
    for copy in halos + backs:
        copy.wait_send()
    for copies, stay in outs:
        stay.wait()
        for copy in copies:
            copy.wait()


def shards(members, target):
    channels, rows, cols = target.shape
    bands, sectors = lax.axis_size("lat"), lax.axis_size("lon")
    assert lax.axis_size("mem") == 2 and cols >= 2**LEVELS
    group = 2 * bands
    quota = -(-channels // group)
    chunks = min(CHUNKS, quota)
    spans = [(quota + k) // chunks for k in range(chunks)]
    scales = LEVELS + 1
    nlat, nlon = rows * bands, cols * sectors

    boxes = lat_tables(nlat)
    sums = [float(np.sum(box.astype(np.float64))) for box in boxes]
    inverses = [1.0 / (2.0**s * boxes[s].astype(np.float64)) for s in range(scales)]
    weights = [0.5 * boxes[s].astype(np.float64) / (channels * nlon * sums[s]) for s in range(scales)]
    vectors = np.stack(inverses + weights + [boxes[0].astype(np.float64)]).reshape(-1, rows).tolist()
    factors = [0.5 * nlat / (sums[s] * 2.0**s) for s in range(scales)]

    sizes = (channels, rows, cols, bands, sectors, spans)
    blocks = pltpu.VMEM((group, quota, rows, cols), jnp.float32)
    dma = pltpu.SemaphoreType.DMA
    gradient, loss = pl.pallas_call(
        functools.partial(kernel, sizes, factors, vectors),
        out_shape=(
            jax.ShapeDtypeStruct((group * quota, rows, cols), jnp.float32),
            jax.ShapeDtypeStruct((1, 1), jnp.float32),
        ),
        in_specs=[pl.BlockSpec(memory_space=pltpu.HBM)] * 2,
        out_specs=(pl.BlockSpec(memory_space=pl.ANY), pl.BlockSpec(memory_space=pltpu.SMEM)),
        scratch_shapes=[
            pltpu.VMEM((channels, rows, cols), jnp.float32),
            pltpu.VMEM((channels, rows, cols), jnp.float32),
            pltpu.VMEM((len(vectors), rows, cols), jnp.float32),
            pltpu.VMEM((scales, group, max(spans), rows, cols), jnp.float32),
            blocks, blocks, blocks, blocks, blocks, blocks, blocks,
            pltpu.VMEM((rows, cols), jnp.float32),
            pltpu.VMEM((group, rows, cols), jnp.float32),
            pltpu.VMEM((sectors, rows, cols), jnp.float32),
            dma((2,)),
            dma((chunks, group)), dma((chunks, group)),
            dma((chunks,)), dma((chunks,)),
            dma((chunks,)), dma((chunks,)),
            dma((chunks, group)), dma((chunks, group)), dma((chunks,)),
            dma((group,)), dma((group,)),
            dma((sectors,)), dma((sectors,)),
        ],
        compiler_params=pltpu.CompilerParams(
            collective_id=0, has_side_effects=True, vmem_limit_bytes=32 * 1024 * 1024
        ),
    )(members, target)
    return gradient[None, :channels], loss[0, 0]


def solution(mesh):
    return jax.shard_map(
        shards,
        mesh=mesh,
        in_specs=(P("mem", None, "lat", "lon"), P(None, "lat", "lon")),
        out_specs=(P("mem", None, "lat", "lon"), P()),
        check_vma=False,
    )
```

```python
import functools

import jax
import jax.numpy as jnp
import numpy as np
from jax import lax
from jax.experimental import pallas as pl
from jax.experimental.pallas import tpu as pltpu
from jax.sharding import PartitionSpec as P

LEVELS = 7
SMOOTH_EPS = 0.05
CHUNKS = 2
MESH = pl.DeviceIdType.MESH


def lat_tables(row_count):
    row_index = np.arange(row_count, dtype=np.float32)
    angle = (np.float32(89.875) - np.float32(0.25) * row_index) * np.float32(np.pi / 180.0)
    current = np.cos(angle).astype(np.float32)
    boxes = [current]
    for level in range(LEVELS):
        reach = 2**level
        current = current + np.pad(current, (0, reach))[reach : reach + row_count]
        boxes.append(current)
    return boxes


def kernel(
    sizes, factors, vectors, members_ref, target_ref, grad_ref, loss_ref,
    mem_v, tgt_v, tab_v, slopes, sent, field, east, own_adj, east_adj, west_adj, final,
    total, group_loss, lon_loss,
    in_sem, x_send, x_recv, h_send, h_recv, b_send, b_recv, o_send, o_recv, o_own,
    lg_send, lg_recv, ll_send, ll_recv,
):
    channels, rows, cols, bands, sectors, span, chunks = sizes
    group = 2 * bands
    quota = span * chunks

    def part(k):
        return pl.ds(k * span, span)
    scales = LEVELS + 1
    mem, lat, lon = lax.axis_index("mem"), lax.axis_index("lat"), lax.axis_index("lon")
    me = mem * bands + lat

    def peer(offset):
        index = lax.rem(me + offset, group)
        return index, {"mem": index // bands, "lat": lax.rem(index, bands), "lon": lon}

    def sector(offset):
        return {"mem": mem, "lat": lat, "lon": lax.rem(lon + offset, sectors)}

    loads = [
        pltpu.make_async_copy(members_ref.at[0], mem_v, in_sem.at[0]),
        pltpu.make_async_copy(target_ref, tgt_v, in_sem.at[1]),
    ]
    for load in loads:
        load.start()
    barrier = pltpu.get_barrier_semaphore()
    for offset in range(1, group):
        pl.semaphore_signal(barrier, inc=1, device_id=peer(offset)[1], device_id_type=MESH)
    for offset in range(1, sectors):
        pl.semaphore_signal(barrier, inc=1, device_id=sector(offset), device_id_type=MESH)

    lane = lax.broadcasted_iota(jnp.int32, (rows, cols), 1)
    sub = lax.broadcasted_iota(jnp.int32, (rows, cols), 0)
    zero = jnp.zeros((rows, cols), jnp.float32)
    for i, vector in enumerate(vectors):
        tile = jnp.full((rows, cols), vector[0], jnp.float32)
        for r in range(1, rows):
            tile = jnp.where(sub == r, vector[r], tile)
        tab_v[i] = tile
    for load in loads:
        load.wait()

    def inverse(scale, band):
        return tab_v[scale * bands + band]

    def loss_weight(scale, band):
        return tab_v[(scales + scale) * bands + band]

    def lat_weight(band):
        return tab_v[2 * scales * bands + band]

    own_weight = tab_v[2 * scales * bands + lat]

    def remote(source, target, send, recv, device):
        return pltpu.make_async_remote_copy(
            src_ref=source, dst_ref=target, send_sem=send, recv_sem=recv,
            device_id=device, device_id_type=MESH,
        )

    def exchange(k, offset):
        index, device = peer(offset)
        return remote(sent.at[index, part(k)], field.at[me, part(k)], x_send.at[k, offset], x_recv.at[k, offset], device)

    def halo(k):
        return remote(field.at[:, part(k)], east.at[:, part(k)], h_send.at[k], h_recv.at[k], sector(sectors - 1))

    def back(k):
        return remote(east_adj.at[:, part(k)], west_adj.at[:, part(k)], b_send.at[k], b_recv.at[k], sector(1))

    def place(k):
        return grad_ref.at[pl.ds(me * quota + k * span, span)]

    def result(k, offset):
        index, device = peer(offset)
        return remote(final.at[index, part(k)], place(k), o_send.at[k, offset], o_recv.at[k, offset], device)

    def stay(k):
        return pltpu.make_async_copy(final.at[me, part(k)], place(k), o_own.at[k])

    for k in range(chunks):
        for g in range(group):
            base = g * quota + k * span
            valid = min(max(channels - base, 0), span)
            edge, stop = k * span + valid, (k + 1) * span
            if valid > 0:
                difference = mem_v[base : base + valid] - tgt_v[base : base + valid]
                sent[g, k * span : edge] = difference * own_weight
            if edge < stop:
                sent[g, edge:stop] = jnp.zeros((stop - edge, rows, cols), jnp.float32)
        if k == 0:
            pl.semaphore_wait(barrier, group + sectors - 2)
        for offset in range(1, group):
            exchange(k, offset).start()
        field[me, part(k)] = sent[me, part(k)]

    for k in range(chunks):
        for offset in range(1, group):
            exchange(k, offset).wait_recv()
        halo(k).start()

    def rows_ahead(tiles, reach):
        hops, remain = divmod(reach, rows)
        if hops >= bands:
            return tiles
        at = lambda b: tiles[b] if b < bands else None
        if remain == 0:
            return [t if at(b + hops) is None else t + at(b + hops) for b, t in enumerate(tiles)]
        turned = [pltpu.roll(t, rows - remain, 1) for t in tiles]
        near = sub < rows - remain
        out = []
        for b, t in enumerate(tiles):
            if b + hops >= bands:
                out.append(t)
                continue
            beyond = turned[b + hops + 1] if b + hops + 1 < bands else zero
            out.append(t + jnp.where(near, turned[b + hops], beyond))
        return out

    def rows_behind(tiles, reach):
        hops, remain = divmod(reach, rows)
        if hops >= bands:
            return tiles
        if remain == 0:
            return [t + tiles[b - hops] if b >= hops else t for b, t in enumerate(tiles)]
        turned = [pltpu.roll(t, remain, 1) for t in tiles]
        near = sub >= remain
        out = []
        for b, t in enumerate(tiles):
            if b < hops:
                out.append(t)
                continue
            beyond = turned[b - hops - 1] if b - hops - 1 >= 0 else zero
            out.append(t + jnp.where(near, turned[b - hops], beyond))
        return out

    def absolute(value):
        square = value * value + SMOOTH_EPS * SMOOTH_EPS
        root = lax.rsqrt(square)
        return square * root, value * root

    total[...] = zero

    def work(k):
        own = [[field[m * bands + b, part(k)] for b in range(bands)] for m in range(2)]
        next_ = [[east[m * bands + b, part(k)] for b in range(bands)] for m in range(2)]
        score = jnp.zeros((span, rows, cols), jnp.float32)
        for scale in range(scales):
            if scale > 0:
                reach = 2 ** (scale - 1)
                own = [rows_ahead(t, reach) for t in own]
                next_ = [rows_ahead(t, reach) for t in next_]
                keep = lane < cols - reach
                for m in range(2):
                    for b in range(bands):
                        turned_own = pltpu.roll(own[m][b], cols - reach, 2)
                        turned_next = pltpu.roll(next_[m][b], cols - reach, 2)
                        own[m][b] = own[m][b] + jnp.where(keep, turned_own, turned_next)
                        if scale < LEVELS:
                            next_[m][b] = next_[m][b] + turned_next
            for b in range(bands):
                leader = own[0][b] * inverse(scale, b)
                partner = own[1][b] * inverse(scale, b)
                first_abs, first_slope = absolute(leader)
                second_abs, second_slope = absolute(partner)
                spread_abs, spread_slope = absolute(leader - partner)
                score = score + loss_weight(scale, b) * (first_abs + second_abs - spread_abs)
                slopes[scale, b, 0:span] = (first_slope - spread_slope) * factors[scale]
                slopes[scale, bands + b, 0:span] = (second_slope + spread_slope) * factors[scale]
        mine = [[slopes[LEVELS, m * bands + b, 0:span] for b in range(bands)] for m in range(2)]
        theirs = [[None] * bands for m in range(2)]
        for level in reversed(range(LEVELS)):
            reach = 2**level
            keep = lane >= reach
            for m in range(2):
                for b in range(bands):
                    turned_mine = pltpu.roll(mine[m][b], reach, 2)
                    if level == LEVELS - 1:
                        theirs[m][b] = jnp.where(keep, zero, turned_mine)
                    else:
                        turned_theirs = pltpu.roll(theirs[m][b], reach, 2)
                        theirs[m][b] = theirs[m][b] + jnp.where(keep, turned_theirs, turned_mine)
                    mine[m][b] = mine[m][b] + jnp.where(keep, turned_mine, zero)
            mine = [rows_behind(t, reach) for t in mine]
            theirs = [rows_behind(t, reach) for t in theirs]
            mine = [[mine[m][b] + slopes[level, m * bands + b, 0:span] for b in range(bands)] for m in range(2)]
        for m in range(2):
            for b in range(bands):
                own_adj[m * bands + b, part(k)] = mine[m][b]
                east_adj[m * bands + b, part(k)] = theirs[m][b]
        kept = zero
        for i in range(span):
            kept = kept + score[i] * (me * quota + k * span + i < channels).astype(jnp.float32)
        total[...] += kept

    def finish(k):
        back(k).wait_recv()
        for g in range(group):
            final[g, part(k)] = (own_adj[g, part(k)] + west_adj[g, part(k)]) * lat_weight(g % bands)
        for offset in range(1, group):
            result(k, offset).start()
        stay(k).start()

    def turn(k, carry):
        halo(k).wait_recv()
        work(k)
        back(k).start()

        @pl.when(k > 0)
        def _():
            finish(k - 1)

        return carry

    lax.fori_loop(0, chunks, turn, 0)

    group_loss[me] = total[...]
    group_copies = []
    for offset in range(1, group):
        copy = remote(total, group_loss.at[me], lg_send.at[offset], lg_recv.at[offset], peer(offset)[1])
        copy.start()
        group_copies.append(copy)
    finish(chunks - 1)
    for copy in group_copies:
        copy.wait()
    subtotal = group_loss[0]
    for g in range(1, group):
        subtotal = subtotal + group_loss[g]
    lon_loss[lon] = subtotal
    total[...] = subtotal
    lon_copies = []
    for offset in range(1, sectors):
        copy = remote(total, lon_loss.at[lon], ll_send.at[offset], ll_recv.at[offset], sector(offset))
        copy.start()
        lon_copies.append(copy)
    for copy in lon_copies:
        copy.wait()
    subtotal = lon_loss[0]
    for j in range(1, sectors):
        subtotal = subtotal + lon_loss[j]
    loss_ref[0, 0] = jnp.sum(subtotal)

    for k in range(chunks):
        halo(k).wait_send()
        back(k).wait_send()
        stay(k).wait()
        for offset in range(1, group):
            exchange(k, offset).wait_send()
            result(k, offset).wait()


def shards(members, target):
    channels, rows, cols = target.shape
    bands, sectors = lax.axis_size("lat"), lax.axis_size("lon")
    assert lax.axis_size("mem") == 2 and cols >= 2**LEVELS
    group = 2 * bands
    chunks = CHUNKS
    span = -(-channels // (group * chunks))
    quota = span * chunks
    scales = LEVELS + 1
    nlat, nlon = rows * bands, cols * sectors

    boxes = lat_tables(nlat)
    sums = [float(np.sum(box.astype(np.float64))) for box in boxes]
    inverses = [1.0 / (2.0**s * boxes[s].astype(np.float64)) for s in range(scales)]
    weights = [0.5 * boxes[s].astype(np.float64) / (channels * nlon * sums[s]) for s in range(scales)]
    vectors = np.stack(inverses + weights + [boxes[0].astype(np.float64)]).reshape(-1, rows).tolist()
    factors = [0.5 * nlat / (sums[s] * 2.0**s) for s in range(scales)]

    sizes = (channels, rows, cols, bands, sectors, span, chunks)
    blocks = pltpu.VMEM((group, quota, rows, cols), jnp.float32)
    dma = pltpu.SemaphoreType.DMA
    gradient, loss = pl.pallas_call(
        functools.partial(kernel, sizes, factors, vectors),
        out_shape=(
            jax.ShapeDtypeStruct((group * quota, rows, cols), jnp.float32),
            jax.ShapeDtypeStruct((1, 1), jnp.float32),
        ),
        in_specs=[pl.BlockSpec(memory_space=pl.ANY)] * 2,
        out_specs=(pl.BlockSpec(memory_space=pl.ANY), pl.BlockSpec(memory_space=pltpu.SMEM)),
        scratch_shapes=[
            pltpu.VMEM((channels, rows, cols), jnp.float32),
            pltpu.VMEM((channels, rows, cols), jnp.float32),
            pltpu.VMEM((len(vectors), rows, cols), jnp.float32),
            pltpu.VMEM((scales, group, span, rows, cols), jnp.float32),
            blocks, blocks, blocks, blocks, blocks, blocks, blocks,
            pltpu.VMEM((rows, cols), jnp.float32),
            pltpu.VMEM((group, rows, cols), jnp.float32),
            pltpu.VMEM((sectors, rows, cols), jnp.float32),
            dma((2,)),
            dma((chunks, group)), dma((chunks, group)),
            dma((chunks,)), dma((chunks,)),
            dma((chunks,)), dma((chunks,)),
            dma((chunks, group)), dma((chunks, group)), dma((chunks,)),
            dma((group,)), dma((group,)),
            dma((sectors,)), dma((sectors,)),
        ],
        compiler_params=pltpu.CompilerParams(
            collective_id=0, has_side_effects=True, vmem_limit_bytes=60 * 1024 * 1024
        ),
    )(members, target)
    return gradient[None, :channels], loss[0, 0]


def solution(mesh):
    return jax.shard_map(
        shards,
        mesh=mesh,
        in_specs=(P("mem", None, "lat", "lon"), P(None, "lat", "lon")),
        out_specs=(P("mem", None, "lat", "lon"), P()),
        check_vma=False,
    )
```

```python
import functools

import jax
import jax.numpy as jnp
import numpy as np
from jax import lax
from jax.experimental import pallas as pl
from jax.experimental.pallas import tpu as pltpu
from jax.sharding import PartitionSpec as P

LEVELS = 7
SMOOTH_EPS = 0.05
CELL = 8
MESH = pl.DeviceIdType.MESH


def lat_tables(row_count):
    row_index = np.arange(row_count, dtype=np.float32)
    angle = (np.float32(89.875) - np.float32(0.25) * row_index) * np.float32(np.pi / 180.0)
    current = np.cos(angle).astype(np.float32)
    boxes = [current]
    for level in range(LEVELS):
        reach = 2**level
        current = current + np.pad(current, (0, reach))[reach : reach + row_count]
        boxes.append(current)
    return boxes


def box_matrix(shape, cell, anchor, reach):
    source = lax.broadcasted_iota(jnp.int32, shape, cell)
    start = lax.broadcasted_iota(jnp.int32, shape, anchor)
    inside = jnp.where(source >= start, 1.0, 0.0) * jnp.where(source < start + reach, 1.0, 0.0)
    return inside.astype(jnp.bfloat16)


def split(value, count):
    pieces = []
    for _ in range(count):
        piece = value.astype(jnp.bfloat16)
        pieces.append(piece)
        value = value - piece.astype(jnp.float32)
    return jnp.concatenate(pieces, axis=1)


def rows_ahead(tiles, scale):
    count = len(tiles)
    if 2**scale >= count:
        tiles = list(tiles)
        for r in reversed(range(count - 1)):
            tiles[r] = tiles[r] + tiles[r + 1]
        return tiles
    for level in range(scale):
        reach = 2**level
        tiles = [t + tiles[r + reach] if r + reach < count else t for r, t in enumerate(tiles)]
    return tiles


def rows_behind(tiles, scale):
    return rows_ahead(tiles[::-1], scale)[::-1]


def absolute(value):
    square = value * value + SMOOTH_EPS * SMOOTH_EPS
    root = lax.rsqrt(square)
    return square * root, value * root


def kernel(
    sizes, factors, inverses, weights, lat_weight, members_ref, target_ref, grad_ref, loss_ref,
    mem_v, tgt_v, tab_v, ahead_v, behind_v, lhs, boxes, slopes, flat_slope, adjoint,
    sent, field, east, own_adj, east_adj, west_adj, final,
    total, group_loss, lon_loss,
    in_sem, x_send, x_recv, h_send, h_recv, b_send, b_recv, o_send, o_recv, o_own,
    lg_send, lg_recv, ll_send, ll_recv,
):
    channels, rows, cols, bands, sectors, spans = sizes
    group = 2 * bands
    quota = sum(spans)
    chunks = len(spans)
    nlat = rows * bands
    scales = LEVELS + 1
    mem, lat, lon = lax.axis_index("mem"), lax.axis_index("lat"), lax.axis_index("lon")
    me = mem * bands + lat

    def part(k):
        return pl.ds(k * CELL * rows, spans[k] * rows)

    def peer(offset):
        index = lax.rem(me + offset, group)
        return index, {"mem": index // bands, "lat": lax.rem(index, bands), "lon": lon}

    def sector(offset):
        return {"mem": mem, "lat": lat, "lon": lax.rem(lon + offset, sectors)}

    loads = [
        pltpu.make_async_copy(members_ref.at[0], mem_v, in_sem.at[0]),
        pltpu.make_async_copy(target_ref, tgt_v, in_sem.at[1]),
    ]
    for load in loads:
        load.start()
    barrier = pltpu.get_barrier_semaphore()
    for offset in range(1, group):
        pl.semaphore_signal(barrier, inc=1, device_id=peer(offset)[1], device_id_type=MESH)
    for offset in range(1, sectors):
        pl.semaphore_signal(barrier, inc=1, device_id=sector(offset), device_id_type=MESH)

    sub = lax.broadcasted_iota(jnp.int32, (rows, cols), 0)
    zero = jnp.zeros((rows, cols), jnp.float32)
    for band in range(bands):
        tile = jnp.full((rows, cols), lat_weight[band * rows], jnp.float32)
        for r in range(1, rows):
            tile = jnp.where(sub == r, lat_weight[band * rows + r], tile)
        tab_v[band] = tile
    for load in loads:
        load.wait()
    own_weight = tab_v[lat]

    def remote(source, target, send, recv, device):
        return pltpu.make_async_remote_copy(
            src_ref=source, dst_ref=target, send_sem=send, recv_sem=recv,
            device_id=device, device_id_type=MESH,
        )

    def exchange(k, offset):
        index, device = peer(offset)
        return remote(sent.at[index, part(k)], field.at[me, part(k)], x_send.at[k, offset], x_recv.at[k, offset], device)

    def halo(k):
        return remote(field.at[:, part(k)], east.at[:, part(k)], h_send.at[k], h_recv.at[k], sector(sectors - 1))

    def back(k):
        return remote(east_adj.at[:, part(k)], west_adj.at[:, part(k)], b_send.at[k], b_recv.at[k], sector(1))

    def place(k):
        return grad_ref.at[pl.ds((me * quota + k * CELL) * rows, spans[k] * rows)]

    def result(k, offset):
        index, device = peer(offset)
        return remote(final.at[index, part(k)], place(k), o_send.at[k, offset], o_recv.at[k, offset], device)

    def stay(k):
        return pltpu.make_async_copy(final.at[me, part(k)], place(k), o_own.at[k])

    for k in range(chunks):
        for g in range(group):
            base = g * quota + k * CELL
            valid = min(max(channels - base, 0), spans[k])
            start, edge, stop = k * CELL, k * CELL + valid, k * CELL + spans[k]
            if valid > 0:
                difference = mem_v[base : base + valid] - tgt_v[base : base + valid]
                sent[g, start * rows : edge * rows] = (difference * own_weight).reshape(valid * rows, cols)
            if edge < stop:
                sent[g, edge * rows : stop * rows] = jnp.zeros(((stop - edge) * rows, cols), jnp.float32)
        if k == 0:
            pl.semaphore_wait(barrier, group + sectors - 2)
        for offset in range(1, group):
            exchange(k, offset).start()
        field[me, part(k)] = sent[me, part(k)]

    for scale in range(1, scales):
        at = pl.ds((scale - 1) * cols, cols)
        matrix = box_matrix((2 * cols, cols), 0, 1, 2**scale)
        for piece in range(3):
            ahead_v[pl.ds(piece * 2 * cols, 2 * cols), at] = matrix
        matrix = box_matrix((cols, 2 * cols), 1, 0, 2**scale)
        for piece in range(2):
            behind_v[pl.ds((piece * LEVELS + scale - 1) * cols, cols), :] = matrix
    spare = chunks * CELL - quota
    if spare > 0:
        for buffer in (field, east):
            buffer[:, quota * rows : chunks * CELL * rows] = jnp.zeros((group, spare * rows, cols), jnp.float32)

    for k in range(chunks):
        for offset in range(1, group):
            exchange(k, offset).wait_recv()
        halo(k).start()

    total[...] = zero

    def strided(k, r):
        return pl.ds(k * CELL * rows + r, CELL, stride=rows)

    def tile(m, row):
        return pl.ds((m * nlat + row) * CELL, CELL)

    def work(k):
        for m in range(2):
            for row in range(nlat):
                band, r = divmod(row, rows)
                lhs[tile(m, row), 0:cols] = field[m * bands + band, strided(k, r), :]
                lhs[tile(m, row), cols : 2 * cols] = east[m * bands + band, strided(k, r), :]
        boxes[...] = jnp.dot(split(lhs[...], 3), ahead_v[...], preferred_element_type=jnp.float32)
        score = jnp.zeros((CELL, cols), jnp.float32)
        for scale in range(scales):
            at = pl.ds((scale - 1) * cols, cols)
            fields = []
            for m in range(2):
                if scale == 0:
                    fields.append([lhs[tile(m, row), 0:cols] for row in range(nlat)])
                else:
                    fields.append(rows_ahead([boxes[tile(m, row), at] for row in range(nlat)], scale))
            slope = [[], []]
            for row in range(nlat):
                leader = fields[0][row] * inverses[scale][row]
                partner = fields[1][row] * inverses[scale][row]
                first_abs, first_slope = absolute(leader)
                second_abs, second_slope = absolute(partner)
                spread_abs, spread_slope = absolute(leader - partner)
                score = score + weights[scale][row] * (first_abs + second_abs - spread_abs)
                slope[0].append((first_slope - spread_slope) * factors[scale])
                slope[1].append((second_slope + spread_slope) * factors[scale])
            for m in range(2):
                if scale == 0:
                    for row in range(nlat):
                        flat_slope[tile(m, row), :] = slope[m][row]
                else:
                    for row, value in enumerate(rows_behind(slope[m], scale)):
                        slopes[tile(m, row), at] = value
        adjoint[...] = jnp.dot(split(slopes[...], 2), behind_v[...], preferred_element_type=jnp.float32)
        for m in range(2):
            for row in range(nlat):
                band, r = divmod(row, rows)
                own_adj[m * bands + band, strided(k, r), :] = adjoint[tile(m, row), 0:cols] + flat_slope[tile(m, row), :]
                east_adj[m * bands + band, strided(k, r), :] = adjoint[tile(m, row), cols : 2 * cols]
        place_in = k * CELL + lax.broadcasted_iota(jnp.int32, (CELL, cols), 0)
        inside = jnp.where(place_in < quota, 1.0, 0.0) * jnp.where(me * quota + place_in < channels, 1.0, 0.0)
        total[...] += score * inside

    def finish(k):
        back(k).wait_recv()
        for g in range(group):
            summed = (own_adj[g, part(k)] + west_adj[g, part(k)]).reshape(spans[k], rows, cols)
            final[g, part(k)] = (summed * tab_v[g % bands]).reshape(spans[k] * rows, cols)
        for offset in range(1, group):
            result(k, offset).start()
        stay(k).start()

    for k in range(chunks):
        halo(k).wait_recv()
        work(k)
        back(k).start()
        if k > 0:
            finish(k - 1)

    group_loss[me] = total[...]
    group_copies = []
    for offset in range(1, group):
        copy = remote(total, group_loss.at[me], lg_send.at[offset], lg_recv.at[offset], peer(offset)[1])
        copy.start()
        group_copies.append(copy)
    finish(chunks - 1)
    for copy in group_copies:
        copy.wait()
    subtotal = group_loss[0]
    for g in range(1, group):
        subtotal = subtotal + group_loss[g]
    lon_loss[lon] = subtotal
    total[...] = subtotal
    lon_copies = []
    for offset in range(1, sectors):
        copy = remote(total, lon_loss.at[lon], ll_send.at[offset], ll_recv.at[offset], sector(offset))
        copy.start()
        lon_copies.append(copy)
    for copy in lon_copies:
        copy.wait()
    subtotal = lon_loss[0]
    for j in range(1, sectors):
        subtotal = subtotal + lon_loss[j]
    loss_ref[0, 0] = jnp.sum(subtotal)

    for k in range(chunks):
        halo(k).wait_send()
        back(k).wait_send()
        stay(k).wait()
        for offset in range(1, group):
            exchange(k, offset).wait_send()
            result(k, offset).wait()


def shards(members, target):
    channels, rows, cols = target.shape
    bands, sectors = lax.axis_size("lat"), lax.axis_size("lon")
    assert lax.axis_size("mem") == 2 and cols >= 2**LEVELS
    group = 2 * bands
    quota = -(-channels // group)
    chunks = -(-quota // CELL)
    spans = [min(CELL, quota - k * CELL) for k in range(chunks)]
    scales = LEVELS + 1
    nlat, nlon = rows * bands, cols * sectors

    boxes = lat_tables(nlat)
    sums = [float(np.sum(box.astype(np.float64))) for box in boxes]
    inverses = [(1.0 / (2.0**s * boxes[s].astype(np.float64))).tolist() for s in range(scales)]
    weights = [(0.5 * boxes[s].astype(np.float64) / (channels * nlon * sums[s])).tolist() for s in range(scales)]
    factors = [0.5 * nlat / (sums[s] * 2.0**s) for s in range(scales)]

    sizes = (channels, rows, cols, bands, sectors, spans)
    blocks = pltpu.VMEM((group, chunks * CELL * rows, cols), jnp.float32)
    lines = 2 * nlat * CELL
    dma = pltpu.SemaphoreType.DMA
    gradient, loss = pl.pallas_call(
        functools.partial(kernel, sizes, factors, inverses, weights, boxes[0].tolist()),
        out_shape=(
            jax.ShapeDtypeStruct((group * quota * rows, cols), jnp.float32),
            jax.ShapeDtypeStruct((1, 1), jnp.float32),
        ),
        in_specs=[pl.BlockSpec(memory_space=pl.ANY)] * 2,
        out_specs=(pl.BlockSpec(memory_space=pl.ANY), pl.BlockSpec(memory_space=pltpu.SMEM)),
        scratch_shapes=[
            pltpu.VMEM((channels, rows, cols), jnp.float32),
            pltpu.VMEM((channels, rows, cols), jnp.float32),
            pltpu.VMEM((bands, rows, cols), jnp.float32),
            pltpu.VMEM((6 * cols, LEVELS * cols), jnp.bfloat16),
            pltpu.VMEM((2 * LEVELS * cols, 2 * cols), jnp.bfloat16),
            pltpu.VMEM((lines, 2 * cols), jnp.float32),
            pltpu.VMEM((lines, LEVELS * cols), jnp.float32),
            pltpu.VMEM((lines, LEVELS * cols), jnp.float32),
            pltpu.VMEM((lines, cols), jnp.float32),
            pltpu.VMEM((lines, 2 * cols), jnp.float32),
            blocks, blocks, blocks, blocks, blocks, blocks, blocks,
            pltpu.VMEM((rows, cols), jnp.float32),
            pltpu.VMEM((group, rows, cols), jnp.float32),
            pltpu.VMEM((sectors, rows, cols), jnp.float32),
            dma((2,)),
            dma((chunks, group)), dma((chunks, group)),
            dma((chunks,)), dma((chunks,)),
            dma((chunks,)), dma((chunks,)),
            dma((chunks, group)), dma((chunks, group)), dma((chunks,)),
            dma((group,)), dma((group,)),
            dma((sectors,)), dma((sectors,)),
        ],
        compiler_params=pltpu.CompilerParams(
            collective_id=0, has_side_effects=True, vmem_limit_bytes=60 * 1024 * 1024
        ),
    )(members, target)
    return gradient.reshape(1, group * quota, rows, cols)[:, :channels], loss[0, 0]


def solution(mesh):
    return jax.shard_map(
        shards,
        mesh=mesh,
        in_specs=(P("mem", None, "lat", "lon"), P(None, "lat", "lon")),
        out_specs=(P("mem", None, "lat", "lon"), P()),
        check_vma=False,
    )
```

```python
import functools

import jax
import jax.numpy as jnp
import numpy as np
from jax import lax
from jax.experimental import pallas as pl
from jax.experimental.pallas import tpu as pltpu
from jax.sharding import PartitionSpec as P

LEVELS = 7
SMOOTH_EPS = 0.05
CELL = 8
MESH = pl.DeviceIdType.MESH


def lat_tables(row_count):
    row_index = np.arange(row_count, dtype=np.float32)
    angle = (np.float32(89.875) - np.float32(0.25) * row_index) * np.float32(np.pi / 180.0)
    current = np.cos(angle).astype(np.float32)
    boxes = [current]
    for level in range(LEVELS):
        reach = 2**level
        current = current + np.pad(current, (0, reach))[reach : reach + row_count]
        boxes.append(current)
    return boxes


def box_matrix(shape, cell, anchor, reach):
    source = lax.broadcasted_iota(jnp.int32, shape, cell)
    start = lax.broadcasted_iota(jnp.int32, shape, anchor)
    inside = jnp.where(source >= start, 1.0, 0.0) * jnp.where(source < start + reach, 1.0, 0.0)
    return inside.astype(jnp.bfloat16)


def split(value, count):
    pieces = []
    for _ in range(count):
        piece = value.astype(jnp.bfloat16)
        pieces.append(piece)
        value = value - piece.astype(jnp.float32)
    return jnp.concatenate(pieces, axis=1)


def rows_ahead(tiles, scale):
    count = len(tiles)
    if 2**scale >= count:
        tiles = list(tiles)
        for r in reversed(range(count - 1)):
            tiles[r] = tiles[r] + tiles[r + 1]
        return tiles
    for level in range(scale):
        reach = 2**level
        tiles = [t + tiles[r + reach] if r + reach < count else t for r, t in enumerate(tiles)]
    return tiles


def rows_behind(tiles, scale):
    return rows_ahead(tiles[::-1], scale)[::-1]


def absolute(value):
    square = value * value + SMOOTH_EPS * SMOOTH_EPS
    root = lax.rsqrt(square)
    return square * root, value * root


def kernel(
    sizes, factors, inverses, weights, lat_weight, members_ref, target_ref, grad_ref, loss_ref,
    mem_v, tgt_v, tab_v, ahead_v, behind_v, lhs, boxes, slopes, flat_slope, adjoint,
    sent, field, east, own_adj, east_adj, west_adj, final,
    total, group_loss, lon_loss,
    in_sem, x_send, x_recv, h_send, h_recv, b_send, b_recv, o_send, o_recv, o_own,
    lg_send, lg_recv, ll_send, ll_recv,
):
    channels, rows, cols, bands, sectors, spans = sizes
    group = 2 * bands
    quota = sum(spans)
    chunks = len(spans)
    nlat = rows * bands
    scales = LEVELS + 1
    mem, lat, lon = lax.axis_index("mem"), lax.axis_index("lat"), lax.axis_index("lon")
    me = mem * bands + lat

    def part(k):
        return pl.ds(k * CELL * rows, spans[k] * rows)

    def peer(offset):
        index = lax.rem(me + offset, group)
        return index, {"mem": index // bands, "lat": lax.rem(index, bands), "lon": lon}

    def sector(offset):
        return {"mem": mem, "lat": lat, "lon": lax.rem(lon + offset, sectors)}

    loads = [
        pltpu.make_async_copy(members_ref.at[0], mem_v, in_sem.at[0]),
        pltpu.make_async_copy(target_ref, tgt_v, in_sem.at[1]),
    ]
    for load in loads:
        load.start()
    barrier = pltpu.get_barrier_semaphore()
    for offset in range(1, group):
        pl.semaphore_signal(barrier, inc=1, device_id=peer(offset)[1], device_id_type=MESH)
    for offset in range(1, sectors):
        pl.semaphore_signal(barrier, inc=1, device_id=sector(offset), device_id_type=MESH)

    sub = lax.broadcasted_iota(jnp.int32, (rows, cols), 0)
    zero = jnp.zeros((rows, cols), jnp.float32)
    for band in range(bands):
        tile = jnp.full((rows, cols), lat_weight[band * rows], jnp.float32)
        for r in range(1, rows):
            tile = jnp.where(sub == r, lat_weight[band * rows + r], tile)
        tab_v[band] = tile
    for load in loads:
        load.wait()
    own_weight = tab_v[lat]

    def remote(source, target, send, recv, device):
        return pltpu.make_async_remote_copy(
            src_ref=source, dst_ref=target, send_sem=send, recv_sem=recv,
            device_id=device, device_id_type=MESH,
        )

    def exchange(k, offset):
        index, device = peer(offset)
        return remote(sent.at[index, part(k)], field.at[me, part(k)], x_send.at[k, offset], x_recv.at[k, offset], device)

    def halo(k):
        return remote(field.at[:, part(k)], east.at[:, part(k)], h_send.at[k], h_recv.at[k], sector(sectors - 1))

    def back(k):
        return remote(east_adj.at[:, part(k)], west_adj.at[:, part(k)], b_send.at[k], b_recv.at[k], sector(1))

    def place(k):
        return grad_ref.at[pl.ds((me * quota + k * CELL) * rows, spans[k] * rows)]

    def result(k, offset):
        index, device = peer(offset)
        return remote(final.at[index, part(k)], place(k), o_send.at[k, offset], o_recv.at[k, offset], device)

    def stay(k):
        return pltpu.make_async_copy(final.at[me, part(k)], place(k), o_own.at[k])

    for k in range(chunks):
        for g in range(group):
            base = g * quota + k * CELL
            valid = min(max(channels - base, 0), spans[k])
            start, edge, stop = k * CELL, k * CELL + valid, k * CELL + spans[k]
            if valid > 0:
                difference = mem_v[base : base + valid] - tgt_v[base : base + valid]
                sent[g, start * rows : edge * rows] = (difference * own_weight).reshape(valid * rows, cols)
            if edge < stop:
                sent[g, edge * rows : stop * rows] = jnp.zeros(((stop - edge) * rows, cols), jnp.float32)
        if k == 0:
            pl.semaphore_wait(barrier, group + sectors - 2)
            for offset in range(1, group):
                exchange(k, offset).start()
        field[me, part(k)] = sent[me, part(k)]

    for scale in range(1, scales):
        at = pl.ds((scale - 1) * cols, cols)
        matrix = box_matrix((2 * cols, cols), 0, 1, 2**scale)
        for piece in range(3):
            ahead_v[pl.ds(piece * 2 * cols, 2 * cols), at] = matrix
        matrix = box_matrix((cols, 2 * cols), 1, 0, 2**scale)
        for piece in range(2):
            behind_v[pl.ds((piece * LEVELS + scale - 1) * cols, cols), :] = matrix
    spare = chunks * CELL - quota
    if spare > 0:
        for buffer in (field, east):
            buffer[:, quota * rows : chunks * CELL * rows] = jnp.zeros((group, spare * rows, cols), jnp.float32)

    for k in range(chunks):
        for offset in range(1, group):
            exchange(k, offset).wait_recv()
        if k + 1 < chunks:
            for offset in range(1, group):
                exchange(k + 1, offset).start()
        halo(k).start()

    total[...] = zero

    def strided(k, r):
        return pl.ds(k * CELL * rows + r, CELL, stride=rows)

    def tile(m, row):
        return pl.ds((m * nlat + row) * CELL, CELL)

    def work(k):
        for m in range(2):
            for row in range(nlat):
                band, r = divmod(row, rows)
                lhs[tile(m, row), 0:cols] = field[m * bands + band, strided(k, r), :]
                lhs[tile(m, row), cols : 2 * cols] = east[m * bands + band, strided(k, r), :]
        boxes[...] = jnp.dot(split(lhs[...], 3), ahead_v[...], preferred_element_type=jnp.float32)
        score = jnp.zeros((CELL, cols), jnp.float32)
        for scale in range(scales):
            at = pl.ds((scale - 1) * cols, cols)
            fields = []
            for m in range(2):
                if scale == 0:
                    fields.append([lhs[tile(m, row), 0:cols] for row in range(nlat)])
                else:
                    fields.append(rows_ahead([boxes[tile(m, row), at] for row in range(nlat)], scale))
            slope = [[], []]
            for row in range(nlat):
                leader = fields[0][row] * inverses[scale][row]
                partner = fields[1][row] * inverses[scale][row]
                first_abs, first_slope = absolute(leader)
                second_abs, second_slope = absolute(partner)
                spread_abs, spread_slope = absolute(leader - partner)
                score = score + weights[scale][row] * (first_abs + second_abs - spread_abs)
                slope[0].append((first_slope - spread_slope) * factors[scale])
                slope[1].append((second_slope + spread_slope) * factors[scale])
            for m in range(2):
                if scale == 0:
                    for row in range(nlat):
                        flat_slope[tile(m, row), :] = slope[m][row]
                else:
                    for row, value in enumerate(rows_behind(slope[m], scale)):
                        slopes[tile(m, row), at] = value
        adjoint[...] = jnp.dot(split(slopes[...], 2), behind_v[...], preferred_element_type=jnp.float32)
        for m in range(2):
            for row in range(nlat):
                band, r = divmod(row, rows)
                own_adj[m * bands + band, strided(k, r), :] = adjoint[tile(m, row), 0:cols] + flat_slope[tile(m, row), :]
                east_adj[m * bands + band, strided(k, r), :] = adjoint[tile(m, row), cols : 2 * cols]
        place_in = k * CELL + lax.broadcasted_iota(jnp.int32, (CELL, cols), 0)
        inside = jnp.where(place_in < quota, 1.0, 0.0) * jnp.where(me * quota + place_in < channels, 1.0, 0.0)
        total[...] += score * inside

    def finish(k):
        back(k).wait_recv()
        for g in range(group):
            summed = (own_adj[g, part(k)] + west_adj[g, part(k)]).reshape(spans[k], rows, cols)
            final[g, part(k)] = (summed * tab_v[g % bands]).reshape(spans[k] * rows, cols)
        for offset in range(1, group):
            result(k, offset).start()
        stay(k).start()

    for k in range(chunks):
        halo(k).wait_recv()
        work(k)
        back(k).start()
        if k + 1 == chunks:
            group_loss[me] = total[...]
            group_copies = []
            for offset in range(1, group):
                copy = remote(total, group_loss.at[me], lg_send.at[offset], lg_recv.at[offset], peer(offset)[1])
                copy.start()
                group_copies.append(copy)
        if k > 0:
            finish(k - 1)

    for copy in group_copies:
        copy.wait()
    subtotal = group_loss[0]
    for g in range(1, group):
        subtotal = subtotal + group_loss[g]
    lon_loss[lon] = subtotal
    total[...] = subtotal
    lon_copies = []
    for offset in range(1, sectors):
        copy = remote(total, lon_loss.at[lon], ll_send.at[offset], ll_recv.at[offset], sector(offset))
        copy.start()
        lon_copies.append(copy)
    finish(chunks - 1)
    for copy in lon_copies:
        copy.wait()
    subtotal = lon_loss[0]
    for j in range(1, sectors):
        subtotal = subtotal + lon_loss[j]
    loss_ref[0, 0] = jnp.sum(subtotal)

    for k in range(chunks):
        halo(k).wait_send()
        back(k).wait_send()
        stay(k).wait()
        for offset in range(1, group):
            exchange(k, offset).wait_send()
            result(k, offset).wait()


def shards(members, target):
    channels, rows, cols = target.shape
    bands, sectors = lax.axis_size("lat"), lax.axis_size("lon")
    assert lax.axis_size("mem") == 2 and cols >= 2**LEVELS
    group = 2 * bands
    quota = -(-channels // group)
    chunks = -(-quota // CELL)
    spans = [min(CELL, quota - k * CELL) for k in range(chunks)]
    scales = LEVELS + 1
    nlat, nlon = rows * bands, cols * sectors

    boxes = lat_tables(nlat)
    sums = [float(np.sum(box.astype(np.float64))) for box in boxes]
    inverses = [(1.0 / (2.0**s * boxes[s].astype(np.float64))).tolist() for s in range(scales)]
    weights = [(0.5 * boxes[s].astype(np.float64) / (channels * nlon * sums[s])).tolist() for s in range(scales)]
    factors = [0.5 * nlat / (sums[s] * 2.0**s) for s in range(scales)]

    sizes = (channels, rows, cols, bands, sectors, spans)
    blocks = pltpu.VMEM((group, chunks * CELL * rows, cols), jnp.float32)
    lines = 2 * nlat * CELL
    dma = pltpu.SemaphoreType.DMA
    gradient, loss = pl.pallas_call(
        functools.partial(kernel, sizes, factors, inverses, weights, boxes[0].tolist()),
        out_shape=(
            jax.ShapeDtypeStruct((group * quota * rows, cols), jnp.float32),
            jax.ShapeDtypeStruct((1, 1), jnp.float32),
        ),
        in_specs=[pl.BlockSpec(memory_space=pl.ANY)] * 2,
        out_specs=(pl.BlockSpec(memory_space=pl.ANY), pl.BlockSpec(memory_space=pltpu.SMEM)),
        scratch_shapes=[
            pltpu.VMEM((channels, rows, cols), jnp.float32),
            pltpu.VMEM((channels, rows, cols), jnp.float32),
            pltpu.VMEM((bands, rows, cols), jnp.float32),
            pltpu.VMEM((6 * cols, LEVELS * cols), jnp.bfloat16),
            pltpu.VMEM((2 * LEVELS * cols, 2 * cols), jnp.bfloat16),
            pltpu.VMEM((lines, 2 * cols), jnp.float32),
            pltpu.VMEM((lines, LEVELS * cols), jnp.float32),
            pltpu.VMEM((lines, LEVELS * cols), jnp.float32),
            pltpu.VMEM((lines, cols), jnp.float32),
            pltpu.VMEM((lines, 2 * cols), jnp.float32),
            blocks, blocks, blocks, blocks, blocks, blocks, blocks,
            pltpu.VMEM((rows, cols), jnp.float32),
            pltpu.VMEM((group, rows, cols), jnp.float32),
            pltpu.VMEM((sectors, rows, cols), jnp.float32),
            dma((2,)),
            dma((chunks, group)), dma((chunks, group)),
            dma((chunks,)), dma((chunks,)),
            dma((chunks,)), dma((chunks,)),
            dma((chunks, group)), dma((chunks, group)), dma((chunks,)),
            dma((group,)), dma((group,)),
            dma((sectors,)), dma((sectors,)),
        ],
        compiler_params=pltpu.CompilerParams(
            collective_id=0, has_side_effects=True, vmem_limit_bytes=60 * 1024 * 1024
        ),
    )(members, target)
    return gradient.reshape(1, group * quota, rows, cols)[:, :channels], loss[0, 0]


def solution(mesh):
    return jax.shard_map(
        shards,
        mesh=mesh,
        in_specs=(P("mem", None, "lat", "lon"), P(None, "lat", "lon")),
        out_specs=(P("mem", None, "lat", "lon"), P()),
        check_vma=False,
    )
```

```python
import functools

import jax
import jax.numpy as jnp
import numpy as np
from jax import lax
from jax.experimental import pallas as pl
from jax.experimental.pallas import tpu as pltpu
from jax.sharding import PartitionSpec as P

LEVELS = 7
SMOOTH_EPS = 0.05
CELL = 8
MESH = pl.DeviceIdType.MESH


def lat_tables(row_count):
    row_index = np.arange(row_count, dtype=np.float32)
    angle = (np.float32(89.875) - np.float32(0.25) * row_index) * np.float32(np.pi / 180.0)
    current = np.cos(angle).astype(np.float32)
    boxes = [current]
    for level in range(LEVELS):
        reach = 2**level
        current = current + np.pad(current, (0, reach))[reach : reach + row_count]
        boxes.append(current)
    return boxes


def box_matrix(shape, cell, anchor, reach):
    source = lax.broadcasted_iota(jnp.int32, shape, cell)
    start = lax.broadcasted_iota(jnp.int32, shape, anchor)
    inside = jnp.where(source >= start, 1.0, 0.0) * jnp.where(source < start + reach, 1.0, 0.0)
    return inside.astype(jnp.bfloat16)


def split(value, count):
    pieces = []
    for _ in range(count):
        piece = value.astype(jnp.bfloat16)
        pieces.append(piece)
        value = value - piece.astype(jnp.float32)
    return jnp.concatenate(pieces, axis=1)


def rows_ahead(tiles, scale):
    count = len(tiles)
    if 2**scale >= count:
        tiles = list(tiles)
        for r in reversed(range(count - 1)):
            tiles[r] = tiles[r] + tiles[r + 1]
        return tiles
    for level in range(scale):
        reach = 2**level
        tiles = [t + tiles[r + reach] if r + reach < count else t for r, t in enumerate(tiles)]
    return tiles


def rows_behind(tiles, scale):
    return rows_ahead(tiles[::-1], scale)[::-1]


def absolute(value):
    square = value * value + SMOOTH_EPS * SMOOTH_EPS
    root = lax.rsqrt(square)
    return square * root, value * root


def kernel(
    sizes, factors, inverses, weights, lat_weight, members_ref, target_ref, grad_ref, loss_ref,
    mem_v, tgt_v, tab_v, ahead_v, behind_v, lhs, boxes, slopes, flat_slope, adjoint,
    sent, field, east, own_adj, east_adj, west_adj, final,
    total, group_loss, lon_loss,
    in_sem, x_send, x_recv, h_send, h_recv, b_send, b_recv, o_send, o_recv, o_own,
    lg_send, lg_recv, ll_send, ll_recv,
):
    channels, rows, cols, bands, sectors, spans = sizes
    group = 2 * bands
    quota = sum(spans)
    chunks = len(spans)
    nlat = rows * bands
    scales = LEVELS + 1
    mem, lat, lon = lax.axis_index("mem"), lax.axis_index("lat"), lax.axis_index("lon")
    me = mem * bands + lat

    def part(k):
        return pl.ds(k * CELL * rows, spans[k] * rows)

    def peer(offset):
        index = lax.rem(me + offset, group)
        return index, {"mem": index // bands, "lat": lax.rem(index, bands), "lon": lon}

    def sector(offset):
        return {"mem": mem, "lat": lat, "lon": lax.rem(lon + offset, sectors)}

    loads = [
        pltpu.make_async_copy(members_ref.at[0], mem_v, in_sem.at[0]),
        pltpu.make_async_copy(target_ref, tgt_v, in_sem.at[1]),
    ]
    for load in loads:
        load.start()
    barrier = pltpu.get_barrier_semaphore()
    for offset in range(1, group):
        pl.semaphore_signal(barrier, inc=1, device_id=peer(offset)[1], device_id_type=MESH)
    for offset in range(1, sectors):
        pl.semaphore_signal(barrier, inc=1, device_id=sector(offset), device_id_type=MESH)

    sub = lax.broadcasted_iota(jnp.int32, (rows, cols), 0)
    zero = jnp.zeros((rows, cols), jnp.float32)
    for band in range(bands):
        tile = jnp.full((rows, cols), lat_weight[band * rows], jnp.float32)
        for r in range(1, rows):
            tile = jnp.where(sub == r, lat_weight[band * rows + r], tile)
        tab_v[band] = tile
    for load in loads:
        load.wait()
    own_weight = tab_v[lat]

    def remote(source, target, send, recv, device):
        return pltpu.make_async_remote_copy(
            src_ref=source, dst_ref=target, send_sem=send, recv_sem=recv,
            device_id=device, device_id_type=MESH,
        )

    def exchange(k, offset):
        index, device = peer(offset)
        return remote(sent.at[index, part(k)], field.at[me, part(k)], x_send.at[k, offset], x_recv.at[k, offset], device)

    def halo(k, offset):
        index = lax.rem(me + group - offset, group)
        return remote(
            field.at[index, part(k)], east.at[index, part(k)], h_send.at[k, offset], h_recv.at[k, offset],
            sector(sectors - 1),
        )

    def back(k):
        return remote(east_adj.at[:, part(k)], west_adj.at[:, part(k)], b_send.at[k], b_recv.at[k], sector(1))

    def place(k):
        return grad_ref.at[pl.ds((me * quota + k * CELL) * rows, spans[k] * rows)]

    def result(k, offset):
        index, device = peer(offset)
        return remote(final.at[index, part(k)], place(k), o_send.at[k, offset], o_recv.at[k, offset], device)

    def stay(k):
        return pltpu.make_async_copy(final.at[me, part(k)], place(k), o_own.at[k])

    for k in range(chunks):
        for g in range(group):
            base = g * quota + k * CELL
            valid = min(max(channels - base, 0), spans[k])
            start, edge, stop = k * CELL, k * CELL + valid, k * CELL + spans[k]
            if valid > 0:
                difference = mem_v[base : base + valid] - tgt_v[base : base + valid]
                sent[g, start * rows : edge * rows] = (difference * own_weight).reshape(valid * rows, cols)
            if edge < stop:
                sent[g, edge * rows : stop * rows] = jnp.zeros(((stop - edge) * rows, cols), jnp.float32)
        if k == 0:
            pl.semaphore_wait(barrier, group + sectors - 2)
        for offset in range(1, group):
            exchange(k, offset).start()
        field[me, part(k)] = sent[me, part(k)]
        halo(k, 0).start()

    for scale in range(1, scales):
        at = pl.ds((scale - 1) * cols, cols)
        matrix = box_matrix((2 * cols, cols), 0, 1, 2**scale)
        for piece in range(3):
            ahead_v[pl.ds(piece * 2 * cols, 2 * cols), at] = matrix
        matrix = box_matrix((cols, 2 * cols), 1, 0, 2**scale)
        for piece in range(2):
            behind_v[pl.ds((piece * LEVELS + scale - 1) * cols, cols), :] = matrix
    spare = chunks * CELL - quota
    if spare > 0:
        for buffer in (field, east):
            buffer[:, quota * rows : chunks * CELL * rows] = jnp.zeros((group, spare * rows, cols), jnp.float32)

    for k in range(chunks):
        for offset in [group // 2] + [o for o in range(1, group) if o != group // 2]:
            exchange(k, offset).wait_recv()
            halo(k, offset).start()

    total[...] = zero

    def strided(k, r):
        return pl.ds(k * CELL * rows + r, CELL, stride=rows)

    def tile(m, row):
        return pl.ds((m * nlat + row) * CELL, CELL)

    def work(k):
        for m in range(2):
            for row in range(nlat):
                band, r = divmod(row, rows)
                lhs[tile(m, row), 0:cols] = field[m * bands + band, strided(k, r), :]
                lhs[tile(m, row), cols : 2 * cols] = east[m * bands + band, strided(k, r), :]
        boxes[...] = jnp.dot(split(lhs[...], 3), ahead_v[...], preferred_element_type=jnp.float32)
        score = jnp.zeros((CELL, cols), jnp.float32)
        for scale in range(scales):
            at = pl.ds((scale - 1) * cols, cols)
            fields = []
            for m in range(2):
                if scale == 0:
                    fields.append([lhs[tile(m, row), 0:cols] for row in range(nlat)])
                else:
                    fields.append(rows_ahead([boxes[tile(m, row), at] for row in range(nlat)], scale))
            slope = [[], []]
            for row in range(nlat):
                leader = fields[0][row] * inverses[scale][row]
                partner = fields[1][row] * inverses[scale][row]
                first_abs, first_slope = absolute(leader)
                second_abs, second_slope = absolute(partner)
                spread_abs, spread_slope = absolute(leader - partner)
                score = score + weights[scale][row] * (first_abs + second_abs - spread_abs)
                slope[0].append((first_slope - spread_slope) * factors[scale])
                slope[1].append((second_slope + spread_slope) * factors[scale])
            for m in range(2):
                if scale == 0:
                    for row in range(nlat):
                        flat_slope[tile(m, row), :] = slope[m][row]
                else:
                    for row, value in enumerate(rows_behind(slope[m], scale)):
                        slopes[tile(m, row), at] = value
        adjoint[...] = jnp.dot(split(slopes[...], 2), behind_v[...], preferred_element_type=jnp.float32)
        for m in range(2):
            for row in range(nlat):
                band, r = divmod(row, rows)
                own_adj[m * bands + band, strided(k, r), :] = adjoint[tile(m, row), 0:cols] + flat_slope[tile(m, row), :]
                east_adj[m * bands + band, strided(k, r), :] = adjoint[tile(m, row), cols : 2 * cols]
        place_in = k * CELL + lax.broadcasted_iota(jnp.int32, (CELL, cols), 0)
        inside = jnp.where(place_in < quota, 1.0, 0.0) * jnp.where(me * quota + place_in < channels, 1.0, 0.0)
        total[...] += score * inside

    def finish(k):
        back(k).wait_recv()
        for g in range(group):
            summed = (own_adj[g, part(k)] + west_adj[g, part(k)]).reshape(spans[k], rows, cols)
            final[g, part(k)] = (summed * tab_v[g % bands]).reshape(spans[k] * rows, cols)
        for offset in range(1, group):
            result(k, offset).start()
        stay(k).start()

    for k in range(chunks):
        for offset in range(group):
            halo(k, offset).wait_recv()
        work(k)
        back(k).start()
        if k + 1 == chunks:
            group_loss[me] = total[...]
            group_copies = []
            for offset in range(1, group):
                copy = remote(total, group_loss.at[me], lg_send.at[offset], lg_recv.at[offset], peer(offset)[1])
                copy.start()
                group_copies.append(copy)
        if k > 0:
            finish(k - 1)

    for copy in group_copies:
        copy.wait()
    subtotal = group_loss[0]
    for g in range(1, group):
        subtotal = subtotal + group_loss[g]
    lon_loss[lon] = subtotal
    total[...] = subtotal
    lon_copies = []
    for offset in range(1, sectors):
        copy = remote(total, lon_loss.at[lon], ll_send.at[offset], ll_recv.at[offset], sector(offset))
        copy.start()
        lon_copies.append(copy)
    finish(chunks - 1)
    for copy in lon_copies:
        copy.wait()
    subtotal = lon_loss[0]
    for j in range(1, sectors):
        subtotal = subtotal + lon_loss[j]
    loss_ref[0, 0] = jnp.sum(subtotal)

    for k in range(chunks):
        for offset in range(group):
            halo(k, offset).wait_send()
        back(k).wait_send()
        stay(k).wait()
        for offset in range(1, group):
            exchange(k, offset).wait_send()
            result(k, offset).wait()


def shards(members, target):
    channels, rows, cols = target.shape
    bands, sectors = lax.axis_size("lat"), lax.axis_size("lon")
    assert lax.axis_size("mem") == 2 and cols >= 2**LEVELS
    group = 2 * bands
    quota = -(-channels // group)
    chunks = -(-quota // CELL)
    spans = [min(CELL, quota - k * CELL) for k in range(chunks)]
    scales = LEVELS + 1
    nlat, nlon = rows * bands, cols * sectors

    boxes = lat_tables(nlat)
    sums = [float(np.sum(box.astype(np.float64))) for box in boxes]
    inverses = [(1.0 / (2.0**s * boxes[s].astype(np.float64))).tolist() for s in range(scales)]
    weights = [(0.5 * boxes[s].astype(np.float64) / (channels * nlon * sums[s])).tolist() for s in range(scales)]
    factors = [0.5 * nlat / (sums[s] * 2.0**s) for s in range(scales)]

    sizes = (channels, rows, cols, bands, sectors, spans)
    blocks = pltpu.VMEM((group, chunks * CELL * rows, cols), jnp.float32)
    lines = 2 * nlat * CELL
    dma = pltpu.SemaphoreType.DMA
    gradient, loss = pl.pallas_call(
        functools.partial(kernel, sizes, factors, inverses, weights, boxes[0].tolist()),
        out_shape=(
            jax.ShapeDtypeStruct((group * quota * rows, cols), jnp.float32),
            jax.ShapeDtypeStruct((1, 1), jnp.float32),
        ),
        in_specs=[pl.BlockSpec(memory_space=pl.ANY)] * 2,
        out_specs=(pl.BlockSpec(memory_space=pl.ANY), pl.BlockSpec(memory_space=pltpu.SMEM)),
        scratch_shapes=[
            pltpu.VMEM((channels, rows, cols), jnp.float32),
            pltpu.VMEM((channels, rows, cols), jnp.float32),
            pltpu.VMEM((bands, rows, cols), jnp.float32),
            pltpu.VMEM((6 * cols, LEVELS * cols), jnp.bfloat16),
            pltpu.VMEM((2 * LEVELS * cols, 2 * cols), jnp.bfloat16),
            pltpu.VMEM((lines, 2 * cols), jnp.float32),
            pltpu.VMEM((lines, LEVELS * cols), jnp.float32),
            pltpu.VMEM((lines, LEVELS * cols), jnp.float32),
            pltpu.VMEM((lines, cols), jnp.float32),
            pltpu.VMEM((lines, 2 * cols), jnp.float32),
            blocks, blocks, blocks, blocks, blocks, blocks, blocks,
            pltpu.VMEM((rows, cols), jnp.float32),
            pltpu.VMEM((group, rows, cols), jnp.float32),
            pltpu.VMEM((sectors, rows, cols), jnp.float32),
            dma((2,)),
            dma((chunks, group)), dma((chunks, group)),
            dma((chunks, group)), dma((chunks, group)),
            dma((chunks,)), dma((chunks,)),
            dma((chunks, group)), dma((chunks, group)), dma((chunks,)),
            dma((group,)), dma((group,)),
            dma((sectors,)), dma((sectors,)),
        ],
        compiler_params=pltpu.CompilerParams(
            collective_id=0, has_side_effects=True, vmem_limit_bytes=60 * 1024 * 1024
        ),
    )(members, target)
    return gradient.reshape(1, group * quota, rows, cols)[:, :channels], loss[0, 0]


def solution(mesh):
    return jax.shard_map(
        shards,
        mesh=mesh,
        in_specs=(P("mem", None, "lat", "lon"), P(None, "lat", "lon")),
        out_specs=(P("mem", None, "lat", "lon"), P()),
        check_vma=False,
    )
```
